256 devices in a mesh: vol: 4 (over y_hi, core), zs: 64 (over y_lo, x, z).
Axes of the slice: x: 4, y: 4 (y_hi: 2, y_lo: 2; y = y_hi * 2 + y_lo), z: 8, core: 2. Of those that a mesh axis runs over, the one named last changes fastest.
Arguments:
- volume: bfloat16 [64, 1024, 256], P('zs', 'vol'), may hold values from -6 to 6
- first_weight: bfloat16 [9, 12], replicated, may hold values from -3 to 3
- first_offset: float32 [12], replicated, may hold values from -2 to 2
- second_weight: bfloat16 [9, 12, 12], replicated, may hold values from -0.875 to 0.875
- second_offset: float32 [12], replicated, may hold values from -2 to 2
- reduce_conv_weight: bfloat16 [4, 12, 24], replicated, may hold values from -1.25 to 1.25
- reduce_conv_bias: float32 [24], replicated, may hold values from -2 to 2
- deep_weight: bfloat16 [27, 24, 24], replicated, may hold values from -0.3125 to 0.3125
- deep_offset: float32 [24], replicated, may hold values from -2 to 2
Outputs:
- affinity: bfloat16 [64, 24, 512, 128], P(None, None, ('vol', 'zs'))
The draws below stay inside these ranges and needn't reach their ends.
All inputs are finite; a program needn't handle non-finite values.
Results may differ from the reference program's by a relative error of at most 0.0065.
Values may be sent and summed in bfloat16 or wider, within the bound.
A program may use at most 192 MiB of HBM per device.

```python
import jax
import jax.numpy as jnp
from jax import lax

CH_PLANE = 12
CH_DEEP = 24
PY = 256
X = 1024
Z = 64


def block_levels(rng, dims, shards, smallest, top_value):
    level = 1.0
    for position, parts in shards:
        heights = jax.random.uniform(jax.random.fold_in(jax.random.fold_in(rng, 6), position), (parts,), jnp.float32, smallest / len(shards), top_value / len(shards))
        level = level * jnp.repeat(jnp.exp(heights), dims[position] // parts).reshape((-1,) + (1,) * (len(dims) - 1 - position))
    return level


def normal_values(rng, dims, width, limit, split=(), kind=jnp.bfloat16):
    loudness = block_levels(rng, dims, split, -0.22, 0.18) if split else 1.0
    array = jax.random.normal(rng, dims, jnp.float32) * width * loudness
    return jnp.minimum(jnp.maximum(array, -limit), limit).astype(kind)


def setup_inputs(seed: int = 0) -> dict:
    streams_of = jax.random.split(jax.random.key(seed), 10)
    volume = normal_values(streams_of[0], (Z, X, PY), 1.0, 6.0, ((0, 64), (1, 4)))
    first_weight = normal_values(streams_of[1], (9, CH_PLANE), 4 ** -0.5, 3.0)
    first_offset = normal_values(streams_of[2], (CH_PLANE,), 0.5, 2.0, (), jnp.float32)
    second_weight = normal_values(streams_of[3], (9, CH_PLANE, CH_PLANE), 54 ** -0.5, 0.875)
    second_offset = normal_values(streams_of[4], (CH_PLANE,), 0.5, 2.0, (), jnp.float32)
    reduce_conv_weight = normal_values(streams_of[5], (4, CH_PLANE, CH_DEEP), 24 ** -0.5, 1.25)
    reduce_conv_bias = normal_values(streams_of[6], (CH_DEEP,), 0.5, 2.0, (), jnp.float32)
    deep_weight = normal_values(streams_of[7], (27, CH_DEEP, CH_DEEP), 324 ** -0.5, 0.3125)
    deep_offset = normal_values(streams_of[8], (CH_DEEP,), 0.5, 2.0, (), jnp.float32)
    return dict(volume=volume, first_weight=first_weight, first_offset=first_offset, second_weight=second_weight, second_offset=second_offset, reduce_conv_weight=reduce_conv_weight, reduce_conv_bias=reduce_conv_bias, deep_weight=deep_weight, deep_offset=deep_offset)


def plane_conv(field, weight, offset):
    padded = jnp.pad(field, ((0, 0), (1, 1), (1, 1)))
    row_count = field.shape[1]
    col_count = field.shape[2]
    summed = jnp.zeros((weight.shape[2], row_count, col_count), jnp.float32)
    for along_x in range(3):
        for along_y in range(3):
            window = padded[:, along_x:along_x + row_count, along_y:along_y + col_count]
            summed = summed + jnp.einsum("cxy,cd->dxy", window, weight[3 * along_x + along_y])
    return summed + offset[:, None, None]


def reference(volume, first_weight, first_offset, second_weight, second_offset, reduce_conv_weight, reduce_conv_bias, deep_weight, deep_offset):
    plane_chan = first_weight.shape[1]
    deep_chan = reduce_conv_weight.shape[2]
    first_kernel = first_weight.astype(jnp.float32).reshape(9, 1, plane_chan)
    latter_conv_kernel = second_weight.astype(jnp.float32)
    down_kernel = reduce_conv_weight.astype(jnp.float32).reshape(2, 2, plane_chan, deep_chan)
    deep_kernel = deep_weight.astype(jnp.float32)

    def slice_section(plane):
        field = plane.astype(jnp.float32)[None]
        first = jax.nn.relu(plane_conv(field, first_kernel, first_offset)).astype(jnp.bfloat16)
        latter_conv = jax.nn.relu(plane_conv(first.astype(jnp.float32), latter_conv_kernel, second_offset)).astype(jnp.bfloat16)
        half_x = latter_conv.shape[1] // 2
        half_y = latter_conv.shape[2] // 2
        blocks = latter_conv.astype(jnp.float32).reshape(plane_chan, half_x, 2, half_y, 2)
        summed = jnp.einsum("cxayb,abcd->dxy", blocks, down_kernel) + reduce_conv_bias[:, None, None]
        return jax.nn.relu(summed).astype(jnp.bfloat16)

    coarse = lax.map(slice_section, volume)
    padded_depth = jnp.pad(coarse, ((1, 1), (0, 0), (0, 0), (0, 0)))
    row_count = coarse.shape[2]
    col_count = coarse.shape[3]

    def deep_slice(depth_index):
        window = lax.dynamic_slice_in_dim(padded_depth, depth_index, 3, 0).astype(jnp.float32)
        window = jnp.pad(window, ((0, 0), (0, 0), (1, 1), (1, 1)))
        summed = jnp.zeros((deep_chan, row_count, col_count), jnp.float32)
        for along_z in range(3):
            for along_x in range(3):
                for along_y in range(3):
                    piece = window[along_z, :, along_x:along_x + row_count, along_y:along_y + col_count]
                    summed = summed + jnp.einsum("cxy,cd->dxy", piece, deep_kernel[9 * along_z + 3 * along_x + along_y])
        return jax.nn.relu(summed + deep_offset[:, None, None]).astype(jnp.bfloat16)

    return lax.map(deep_slice, jnp.arange(coarse.shape[0], dtype=jnp.int32))
```

```python
import functools

import jax
import jax.numpy as jnp
import numpy as np
from jax import lax
from jax.experimental import pallas as pl
from jax.experimental.pallas import tpu as pltpu
from jax.sharding import PartitionSpec as P

BF16 = jnp.bfloat16
F32 = jnp.float32
MESH = pl.DeviceIdType.MESH
DEPTH = 64
HALF = DEPTH // 2


def tables():
    place1 = np.zeros((3, 256, 12), np.float32)
    mask1 = np.zeros((256, 180), np.float32)
    pick1 = np.zeros((180, 9), np.float32)
    lay1 = np.zeros((180, 72), np.float32)
    source = ({0: (0, 1), 1: (1, 0), 2: (1, 1)}, {0: (1, 0), 1: (1, 1), 2: (2, 0)})
    for parity in range(2):
        for row in range(10):
            kind = parity * 10 + row
            for chan in range(12):
                at = parity * 128 + chan * 10 + row
                place1[0, at, chan] = 1
                place1[1, at, chan] = row >= 3
                place1[2, at, chan] = row < 7
                mask1[at, kind * 9 : kind * 9 + 9] = 1
            for along_x in range(3):
                for along_y in range(3):
                    tap = 3 * along_x + along_y
                    pick1[kind * 9 + tap, tap] = 1
                    shift, origin = source[parity][along_y]
                    fine = row + along_x
                    column = shift * 24 + (fine // 4) * 8 + origin * 4 + fine % 4
                    lay1[kind * 9 + tap, column] = 1
    place2 = np.zeros((96, 12), np.float32)
    lay2 = np.zeros((9, 12, 1024), np.float32)
    block = ({0: 0, 1: 1, 2: 2}, {0: 1, 1: 2, 2: 3})
    for chan in range(12):
        place2[chan * 8 : chan * 8 + 8, chan] = 1
        for along_x in range(3):
            for along_y in range(3):
                for parity in range(2):
                    column = parity * 512 + block[parity][along_y] * 128 + chan * 10 + along_x
                    lay2[3 * along_x + along_y, chan, column] = 1
    place3 = np.zeros((3, 96, 24), np.float32)
    for chan in range(24):
        for row in range(4):
            place3[0, chan * 4 + row, chan] = 1
            place3[1, chan * 4 + row, chan] = row >= 1
            place3[2, chan * 4 + row, chan] = row < 3
    lay3 = np.zeros((4, 12, 256), np.float32)
    for a in range(2):
        for b in range(2):
            for chan in range(12):
                lay3[2 * a + b, chan, b * 96 + chan * 8 + a] = 1
    place4 = np.zeros((48, 24), np.float32)
    lay4 = np.zeros((216, 384), np.float32)
    for chan in range(24):
        place4[chan * 2 : chan * 2 + 2, chan] = 1
        for along_x in range(3):
            for along_y in range(3):
                lay4[along_x * 72 + along_y * 24 + chan, along_y * 96 + chan * 4 + along_x] = 1
    made = (place1, mask1, pick1, lay1, place2, lay2, place3, lay3, place4, lay4)
    return [table.astype(jnp.bfloat16) for table in made]


def mul(a, b):
    return jnp.dot(a, b, preferred_element_type=F32)


def mul_t(a, b):
    return lax.dot_general(a, b, (((1,), (1,)), ((), ())), preferred_element_type=F32)


def column(place, offset):
    summed = jnp.sum(place.astype(F32) * offset, axis=1, keepdims=True)
    return jnp.broadcast_to(summed, (place.shape[0], 128))


def lay_weights(edge, raw, consts, laid):
    w1_ref, o1_ref, w2_ref, o2_ref, w3_ref, o3_ref, w4_ref, o4_ref = raw
    place1, mask1, pick1, lay1, place2, lay2, place3, lay3, place4, lay4 = consts
    m1, b1, m2, b2, m3, b3, m4, b4 = laid

    here1 = place1[edge]
    taps = mul(pick1[...], w1_ref[...]).astype(BF16)
    chosen = mul_t(here1, taps) * mask1[...].astype(F32)
    m1[...] = mul(chosen.astype(BF16), lay1[...]).astype(BF16)
    b1[...] = column(here1, o1_ref[...])

    here2 = place2[...]
    base = jnp.zeros((96, 1024), F32)
    for tap in range(9):
        base = base + mul(mul_t(here2, w2_ref[tap]).astype(BF16), lay2[tap])
    for parity in range(2):
        for block in range(4):
            start = parity * 512 + block * 128
            rows = [
                pltpu.roll(base[8 * c : 8 * c + 8, start : start + 128], 0, 1, stride=1, stride_axis=0)
                for c in range(12)
            ]
            m2[96 * parity : 96 * parity + 96, 128 * block : 128 * block + 128] = jnp.concatenate(
                rows, axis=0
            ).astype(BF16)
    offset2 = column(here2, o2_ref[...])
    b2[:96] = offset2
    b2[96:] = offset2

    here3 = place3[edge]
    base = jnp.zeros((96, 256), F32)
    for tap in range(4):
        base = base + mul(mul_t(here3, w3_ref[tap]).astype(BF16), lay3[tap])
    row = lax.broadcasted_iota(jnp.int32, base.shape, 0) & 3
    placed = base
    for r in range(1, 4):
        placed = jnp.where(row == r, pltpu.roll(base, 2 * r, 1), placed)
    m3[...] = placed[:, :192].astype(BF16)
    b3[...] = column(here3, o3_ref[...])

    here4 = place4[...]
    for dz in range(3):
        base = mul(mul_t(here4, w4_ref[dz]).astype(BF16), lay4[...])
        row = lax.broadcasted_iota(jnp.int32, base.shape, 0) & 1
        placed = jnp.where(row == 1, pltpu.roll(base, 1, 1), base)
        m4[48 * dz : 48 * dz + 48] = placed[:, :288].astype(BF16)
    b4[...] = column(here4, o4_ref[...])


def from_left(value, lane):
    return jnp.where(lane == 0, 0.0, pltpu.roll(value, 1, 1))


def from_right(value, lane):
    return jnp.where(lane == 127, 0.0, pltpu.roll(value, 127, 1))


def both(function, value):
    lane = lax.broadcasted_iota(jnp.int32, (value.shape[0], 128), 1)
    return jnp.concatenate([function(value[:, :128], lane), function(value[:, 128:], lane)], axis=1)


def twice(bias):
    return jnp.concatenate([bias, bias], axis=1)


def relu(value):
    return jnp.maximum(value, 0.0)


def coarse_of(field, laid):
    m1, b1, m2, b2, m3, b3, _, _ = laid
    stacked = jnp.concatenate([both(from_left, field), field, both(from_right, field)], axis=0)
    first = relu(mul(m1[...], stacked.astype(BF16)) + twice(b1[...]))
    even, odd = first[:128], first[128:]
    stacked = jnp.concatenate([both(from_left, odd), even, odd, both(from_right, even)], axis=0)
    second = relu(mul(m2[...], stacked.astype(BF16)) + twice(b2[...])).astype(BF16)
    return relu(mul(m3[...], second) + twice(b3[...]))


def conv_kernel(*refs):
    x_ref, raw, consts, out_ref = refs[0], refs[1:9], refs[9:19], refs[19]
    laid = refs[20:28]
    ahead_ref, lower_ref = refs[28:30]
    position = lax.axis_index("vol") * lax.axis_size("zs") + lax.axis_index("zs")
    last = lax.axis_size("vol") * lax.axis_size("zs") - 1
    edge = jnp.where(position == 0, 1, jnp.where(position == last, 2, 0))
    lay_weights(edge, raw, consts, laid)
    m4, b4 = laid[6:8]

    def step(pair, carry):
        closing, opening = carry
        low = x_ref[pair].astype(F32).reshape(24, 128)
        high = x_ref[pair + HALF].astype(F32).reshape(24, 128)
        coarse = coarse_of(jnp.concatenate([low, high], axis=1), laid)
        stacked = jnp.concatenate([both(from_left, coarse), coarse, both(from_right, coarse)], axis=0)
        deep = mul(m4[...], stacked.astype(BF16))
        total = closing + deep[96:]
        ahead_ref[pair] = deep[96:, 128:]
        lower_ref[pair] = total[:, 128:]
        done = relu(total + twice(b4[...])).astype(BF16)
        slot = jnp.maximum(pair - 1, 0)
        out_ref[slot] = done[:, :128]
        out_ref[slot + HALF] = done[:, 128:]
        return opening + deep[48:96], deep[:48]

    zero = jnp.zeros((48, 256), F32)
    closing, opening = lax.fori_loop(0, HALF, step, (zero, zero), unroll=2)
    bias = b4[...]
    out_ref[HALF - 1] = relu(closing[:, :128] + ahead_ref[0] + bias).astype(BF16)
    out_ref[DEPTH - 1] = relu(closing[:, 128:] + bias).astype(BF16)
    out_ref[HALF] = relu(lower_ref[1] + opening[:, :128] + bias).astype(BF16)


def exchange_kernel(volume_ref, got_ref, tiles, halo_send, halo_recv, send_sem, recv_sem):
    vol, me = lax.axis_index("vol"), lax.axis_index("zs")
    vols, members = lax.axis_size("vol"), lax.axis_size("zs")

    barrier = pltpu.get_barrier_semaphore()

    def greet(step, carry):
        pl.semaphore_signal(
            barrier, inc=1, device_id=(vol, lax.rem(me + step, members)), device_id_type=MESH
        )
        return carry

    @pl.when(vol > 0)
    def _():
        pl.semaphore_signal(barrier, inc=1, device_id=(vol - 1, me), device_id_type=MESH)

    @pl.when(vol < vols - 1)
    def _():
        pl.semaphore_signal(barrier, inc=1, device_id=(vol + 1, me), device_id_type=MESH)

    lax.fori_loop(1, members, greet, 0)

    line = lax.broadcasted_iota(jnp.int32, (256, 256), 0)
    lane = lax.broadcasted_iota(jnp.int32, (256, 256), 1)
    parted = (line == jnp.where(lane < 128, 2 * lane, 2 * lane - 255)).astype(F32).astype(BF16)
    split = mul(volume_ref[0], parted)
    even = split[:, :128].reshape(32, 8, 128)
    odd = split[:, 128:].reshape(32, 8, 128)
    row = lax.broadcasted_iota(jnp.int32, (32, 8, 128), 1)
    upper = jnp.where(row < 4, even, pltpu.roll(odd, 4, 1))
    lower = jnp.where(row < 4, pltpu.roll(even, 4, 1), odd)
    tiles[1:65] = jnp.stack([upper, lower], axis=1).reshape(64, 8, 128).astype(BF16)

    @pl.when(vol == 0)
    def _():
        tiles[0] = jnp.zeros((8, 128), BF16)

    @pl.when(vol == vols - 1)
    def _():
        tiles[65] = jnp.zeros((8, 128), BF16)

    pl.semaphore_wait(
        barrier, members - 1 + jnp.where(vol > 0, 1, 0) + jnp.where(vol < vols - 1, 1, 0)
    )

    def upward():
        return pltpu.make_async_remote_copy(
            src_ref=tiles.at[1],
            dst_ref=tiles.at[65],
            send_sem=halo_send.at[0],
            recv_sem=halo_recv.at[0],
            device_id=(vol - 1, me),
            device_id_type=MESH,
        )

    def downward():
        return pltpu.make_async_remote_copy(
            src_ref=tiles.at[64],
            dst_ref=tiles.at[0],
            send_sem=halo_send.at[1],
            recv_sem=halo_recv.at[1],
            device_id=(vol + 1, me),
            device_id_type=MESH,
        )

    @pl.when(vol > 0)
    def _():
        upward().start()

    @pl.when(vol < vols - 1)
    def _():
        downward().start()

    def give(target):
        pltpu.make_async_remote_copy(
            src_ref=tiles.at[pl.ds(target, 3)],
            dst_ref=got_ref.at[me],
            send_sem=send_sem,
            recv_sem=recv_sem,
            device_id=(vol, target),
            device_id_type=MESH,
        ).start()

    def send(step, carry):
        target = lax.rem(me + step, members)

        @pl.when((target != 0) & (target != members - 1))
        def _():
            give(target)

        return carry

    lax.fori_loop(1, members, send, 0)

    @pl.when(vol < vols - 1)
    def _():
        upward().wait_recv()

    @pl.when(vol > 0)
    def _():
        downward().wait_recv()

    @pl.when(me != 0)
    def _():
        give(0)

    @pl.when(me != members - 1)
    def _():
        give(members - 1)

    got_ref[me] = tiles[pl.ds(me, 3)]

    @pl.when(vol > 0)
    def _():
        upward().wait_send()

    @pl.when(vol < vols - 1)
    def _():
        downward().wait_send()

    rest = got_ref.at[pl.ds(0, 63)]
    pltpu.make_async_copy(rest, rest, send_sem).wait()
    pltpu.make_async_copy(rest, rest, recv_sem).wait()


VMEM = pl.BlockSpec(memory_space=pltpu.VMEM)


def exchange(volume):
    return pl.pallas_call(
        exchange_kernel,
        out_shape=jax.ShapeDtypeStruct((DEPTH, 3, 8, 128), BF16),
        in_specs=[VMEM],
        out_specs=VMEM,
        scratch_shapes=[
            pltpu.VMEM((66, 8, 128), BF16),
            pltpu.SemaphoreType.DMA((2,)),
            pltpu.SemaphoreType.DMA((2,)),
            pltpu.SemaphoreType.DMA,
            pltpu.SemaphoreType.DMA,
        ],
        compiler_params=pltpu.CompilerParams(collective_id=0, has_side_effects=True),
        name="exchange",
    )(volume)


def convolve(gathered, *raw):
    consts = tables()
    return pl.pallas_call(
        conv_kernel,
        out_shape=jax.ShapeDtypeStruct((DEPTH, 48, 128), BF16),
        in_specs=[VMEM] * 19,
        out_specs=VMEM,
        scratch_shapes=[
            pltpu.VMEM((256, 72), BF16),
            pltpu.VMEM((256, 128), F32),
            pltpu.VMEM((192, 512), BF16),
            pltpu.VMEM((192, 128), F32),
            pltpu.VMEM((96, 192), BF16),
            pltpu.VMEM((96, 128), F32),
            pltpu.VMEM((144, 288), BF16),
            pltpu.VMEM((48, 128), F32),
            pltpu.VMEM((HALF, 48, 128), F32),
            pltpu.VMEM((HALF, 48, 128), F32),
        ],
        compiler_params=pltpu.CompilerParams(vmem_limit_bytes=40 * 1024 * 1024),
        name="convolve",
    )(gathered, *raw, *consts)


def shards(volume, w1, o1, w2, o2, w3, o3, w4, o4):
    gathered = exchange(volume)
    done = convolve(
        gathered, w1, o1[None], w2, o2[None], w3, o3[None], w4.reshape(3, 216, 24), o4[None]
    )
    return done.reshape(DEPTH, 24, 2, 128)


def solution(mesh):
    return jax.shard_map(
        shards,
        mesh=mesh,
        in_specs=(P("zs", "vol", None), P(), P(), P(), P(), P(), P(), P(), P()),
        out_specs=P(None, None, ("vol", "zs"), None),
        check_vma=False,
    )
```

```python
import functools

import jax
import jax.numpy as jnp
import numpy as np
from jax import lax
from jax.experimental import pallas as pl
from jax.experimental.pallas import tpu as pltpu
from jax.sharding import PartitionSpec as P

BF16 = jnp.bfloat16
F32 = jnp.float32
MESH = pl.DeviceIdType.MESH
DEPTH = 64
HALF = DEPTH // 2


def tables():
    place1 = np.zeros((3, 256, 12), np.float32)
    mask1 = np.zeros((256, 180), np.float32)
    pick1 = np.zeros((180, 9), np.float32)
    lay1 = np.zeros((180, 72), np.float32)
    source = ({0: (0, 1), 1: (1, 0), 2: (1, 1)}, {0: (1, 0), 1: (1, 1), 2: (2, 0)})
    for parity in range(2):
        for row in range(10):
            kind = parity * 10 + row
            for chan in range(12):
                at = parity * 128 + chan * 10 + row
                place1[0, at, chan] = 1
                place1[1, at, chan] = row >= 3
                place1[2, at, chan] = row < 7
                mask1[at, kind * 9 : kind * 9 + 9] = 1
            for along_x in range(3):
                for along_y in range(3):
                    tap = 3 * along_x + along_y
                    pick1[kind * 9 + tap, tap] = 1
                    shift, origin = source[parity][along_y]
                    fine = row + along_x
                    column = shift * 24 + (fine // 4) * 8 + origin * 4 + fine % 4
                    lay1[kind * 9 + tap, column] = 1
    place2 = np.zeros((96, 12), np.float32)
    lay2 = np.zeros((9, 12, 1024), np.float32)
    block = ({0: 0, 1: 1, 2: 2}, {0: 1, 1: 2, 2: 3})
    for chan in range(12):
        place2[chan * 8 : chan * 8 + 8, chan] = 1
        for along_x in range(3):
            for along_y in range(3):
                for parity in range(2):
                    column = parity * 512 + block[parity][along_y] * 128 + chan * 10 + along_x
                    lay2[3 * along_x + along_y, chan, column] = 1
    place3 = np.zeros((3, 96, 24), np.float32)
    for chan in range(24):
        for row in range(4):
            place3[0, chan * 4 + row, chan] = 1
            place3[1, chan * 4 + row, chan] = row >= 1
            place3[2, chan * 4 + row, chan] = row < 3
    lay3 = np.zeros((12, 4, 256), np.float32)
    for a in range(2):
        for b in range(2):
            for chan in range(12):
                lay3[chan, 2 * a + b, b * 96 + chan * 8 + a] = 1
    place4 = np.zeros((48, 24), np.float32)
    lay4 = np.zeros((24, 27, 1152), np.float32)
    for chan in range(24):
        place4[chan * 2 : chan * 2 + 2, chan] = 1
        for along_z in range(3):
            for along_x in range(3):
                for along_y in range(3):
                    tap = 9 * along_z + 3 * along_x + along_y
                    lay4[chan, tap, along_z * 384 + along_y * 96 + chan * 4 + along_x] = 1
    made = (place1, mask1, pick1, lay1, place2, lay2, place3, lay3, place4, lay4)
    return [table.astype(jnp.bfloat16) for table in made]


def mul(a, b):
    return jnp.dot(a, b, preferred_element_type=F32)


def mul_t(a, b):
    return lax.dot_general(a, b, (((1,), (1,)), ((), ())), preferred_element_type=F32)


def column(place, offset):
    summed = jnp.sum(place.astype(F32) * offset, axis=1, keepdims=True)
    return jnp.broadcast_to(summed, (place.shape[0], 128))


def lay_weights(edge, raw, consts, laid):
    w1_ref, o1_ref, w2_ref, o2_ref, w3_ref, o3_ref, w4_ref, o4_ref = raw
    place1, mask1, pick1, lay1, place2, lay2, place3, lay3, place4, lay4 = consts
    m1, b1, m2, b2, m3, b3, m4, b4 = laid

    here1, here2, here3 = place1[edge], place2[...], place3[edge]
    taps1 = mul(pick1[...], w1_ref[...]).astype(BF16)
    taps2 = [mul_t(here2, w2_ref[tap]).astype(BF16) for tap in range(9)]
    taps3 = [mul_t(here3, w3_ref[chan]).astype(BF16) for chan in range(12)]
    wide4 = sum(mul(w4_ref[chan], lay4[chan]) for chan in range(24)).astype(BF16)

    chosen = mul_t(here1, taps1) * mask1[...].astype(F32)
    base2 = sum(mul(taps2[tap], lay2[tap]) for tap in range(9))
    base3 = sum(mul(taps3[chan], lay3[chan]) for chan in range(12))
    base4 = mul(place4[...], wide4)

    m1[...] = mul(chosen.astype(BF16), lay1[...]).astype(BF16)
    for parity in range(2):
        for block in range(4):
            start = parity * 512 + block * 128
            rows = [
                pltpu.roll(base2[8 * c : 8 * c + 8, start : start + 128], 0, 1, stride=1, stride_axis=0)
                for c in range(12)
            ]
            m2[96 * parity : 96 * parity + 96, 128 * block : 128 * block + 128] = jnp.concatenate(
                rows, axis=0
            ).astype(BF16)
    row = lax.broadcasted_iota(jnp.int32, base3.shape, 0) & 3
    placed = base3
    for r in range(1, 4):
        placed = jnp.where(row == r, pltpu.roll(base3, 2 * r, 1), placed)
    m3[...] = placed[:, :192].astype(BF16)
    row = lax.broadcasted_iota(jnp.int32, base4.shape, 0) & 1
    placed = jnp.where(row == 1, pltpu.roll(base4, 1, 1), base4)
    for dz in range(3):
        m4[48 * dz : 48 * dz + 48] = placed[:, 384 * dz : 384 * dz + 288].astype(BF16)

    b1[...] = column(here1, o1_ref[...])
    offset2 = column(here2, o2_ref[...])
    b2[:96] = offset2
    b2[96:] = offset2
    b3[...] = column(here3, o3_ref[...])
    b4[...] = column(place4[...], o4_ref[...])


def from_left(value, lane):
    return jnp.where(lane == 0, 0.0, pltpu.roll(value, 1, 1))


def from_right(value, lane):
    return jnp.where(lane == 127, 0.0, pltpu.roll(value, 127, 1))


def both(function, value):
    lane = lax.broadcasted_iota(jnp.int32, (value.shape[0], 128), 1)
    return jnp.concatenate([function(value[:, :128], lane), function(value[:, 128:], lane)], axis=1)


def twice(bias):
    return jnp.concatenate([bias, bias], axis=1)


def relu(value):
    return jnp.maximum(value, 0.0)


def convolve_slices(me, arrive, x_ref, laid, held, out_ref):
    m1, b1, m2, b2, m3, b3, m4, b4 = laid
    start_ref, first_ref, second_ref, coarse_ref = held
    groups = HALF // 2

    def step(turn, carry):
        arrive(turn)
        group = jnp.maximum(turn - 3, 0)
        closing, opening = [jnp.where(turn > 3, part, 0.0) for part in carry]
        deep = [mul(m4[...], coarse_ref[half]) for half in range(2)]

        def joined(half, part):
            z = lax.rem(me + 2 * group + half, DEPTH)
            return jnp.concatenate(
                [jnp.where(z == 0, 0.0, part[:, :128]), jnp.where(z == HALF, 0.0, part[:, 128:])], axis=1
            )

        into_before = joined(0, deep[0][96:])
        before = closing + into_before
        here = joined(0, opening) + deep[0][48:96] + joined(1, deep[1][96:])
        start_ref[group, 0] = into_before
        start_ref[group, 1] = here
        bias = twice(b4[...])
        for shift, total in ((DEPTH - 1, before), (0, here)):
            done = relu(total + bias).astype(BF16)
            out_ref[lax.rem(me + 2 * group + shift, DEPTH)] = done[:, :128]
            out_ref[lax.rem(me + 2 * group + shift + HALF, DEPTH)] = done[:, 128:]
        carry = joined(1, deep[0][:48]) + deep[1][48:96], deep[1][:48]

        for half in range(2):
            coarse = relu(mul(m3[...], second_ref[half]) + twice(b3[...]))
            coarse_ref[half, :96] = both(from_left, coarse).astype(BF16)
            coarse_ref[half, 96:192] = coarse.astype(BF16)
            coarse_ref[half, 192:] = both(from_right, coarse).astype(BF16)

        for half in range(2):
            second = relu(mul(m2[...], first_ref[half]) + twice(b2[...]))
            second_ref[half] = second.astype(BF16)

        for half in range(2):
            low = lax.rem(me + 2 * jnp.minimum(turn, groups - 1) + half, DEPTH)
            high = lax.rem(low + HALF, DEPTH)
            field = jnp.concatenate(
                [x_ref[low].astype(F32).reshape(24, 128), x_ref[high].astype(F32).reshape(24, 128)], axis=1
            )
            stacked = jnp.concatenate([both(from_left, field), field, both(from_right, field)], axis=0)
            first = relu(mul(m1[...], stacked.astype(BF16)) + twice(b1[...]))
            even, odd = first[:128], first[128:]
            first_ref[half, :128] = both(from_left, odd).astype(BF16)
            first_ref[half, 128:256] = even.astype(BF16)
            first_ref[half, 256:384] = odd.astype(BF16)
            first_ref[half, 384:] = both(from_right, even).astype(BF16)
        return carry

    zero = jnp.zeros((48, 256), F32)
    closing, opening = lax.fori_loop(0, groups + 3, step, (zero, zero))
    bias = b4[...]
    swap = lambda value: jnp.concatenate([value[:, 128:], value[:, :128]], axis=1)
    opening = swap(opening)
    opening = jnp.concatenate(
        [jnp.where(me == 0, 0.0, opening[:, :128]), jnp.where(me == HALF, 0.0, opening[:, 128:])], axis=1
    )
    ends = ((HALF - 1, closing + swap(start_ref[0, 0])), (0, start_ref[0, 1] + opening))
    for shift, total in ends:
        done = relu(total + twice(bias)).astype(BF16)
        out_ref[lax.rem(me + shift, DEPTH)] = done[:, :128]
        out_ref[lax.rem(me + shift + HALF, DEPTH)] = done[:, 128:]


EARLY = 8


def encoder_kernel(*refs):
    volume_hbm, fetched_hbm, out_ref = refs[0], refs[1:19], refs[19]
    volume_ref, fetched = refs[20], refs[21:39]
    laid, held = refs[39:47], refs[47:51]
    tiles, got_ref = refs[51:53]
    fetch_sem, halo_send, halo_recv, send_sem, recv_sem = refs[53:]
    vol, me = lax.axis_index("vol"), lax.axis_index("zs")
    vols, members = lax.axis_size("vol"), lax.axis_size("zs")

    load = pltpu.make_async_copy(volume_hbm, volume_ref, fetch_sem.at[18])
    load.start()
    loads = [
        pltpu.make_async_copy(source, target, fetch_sem.at[at])
        for at, (source, target) in enumerate(zip(fetched_hbm, fetched))
    ]
    barrier = pltpu.get_barrier_semaphore()

    def greet(step, carry):
        pl.semaphore_signal(
            barrier, inc=1, device_id=(vol, lax.rem(me + step, members)), device_id_type=MESH
        )
        return carry

    @pl.when(vol > 0)
    def _():
        pl.semaphore_signal(barrier, inc=1, device_id=(vol - 1, me), device_id_type=MESH)

    @pl.when(vol < vols - 1)
    def _():
        pl.semaphore_signal(barrier, inc=1, device_id=(vol + 1, me), device_id_type=MESH)

    lax.fori_loop(1, members, greet, 0)
    for each in loads:
        each.start()
    load.wait()

    line = lax.broadcasted_iota(jnp.int32, (256, 256), 0)
    lane = lax.broadcasted_iota(jnp.int32, (256, 256), 1)
    parted = (line == jnp.where(lane < 128, 2 * lane, 2 * lane - 255)).astype(F32).astype(BF16)
    split = mul(volume_ref[0], parted)
    even = split[:, :128].reshape(32, 8, 128)
    odd = split[:, 128:].reshape(32, 8, 128)
    row = lax.broadcasted_iota(jnp.int32, (32, 8, 128), 1)
    upper = jnp.where(row < 4, even, pltpu.roll(odd, 4, 1))
    lower = jnp.where(row < 4, pltpu.roll(even, 4, 1), odd)
    tiles[1:65] = jnp.stack([upper, lower], axis=1).reshape(64, 8, 128).astype(BF16)

    @pl.when(vol == 0)
    def _():
        tiles[0] = jnp.zeros((8, 128), BF16)

    @pl.when(vol == vols - 1)
    def _():
        tiles[65] = jnp.zeros((8, 128), BF16)

    for each in loads:
        each.wait()
    edge = jnp.where(
        (vol == 0) & (me == 0), 1, jnp.where((vol == vols - 1) & (me == members - 1), 2, 0)
    )
    lay_weights(edge, fetched[:8], fetched[8:], laid)

    pl.semaphore_wait(
        barrier, members - 1 + jnp.where(vol > 0, 1, 0) + jnp.where(vol < vols - 1, 1, 0)
    )

    def upward():
        return pltpu.make_async_remote_copy(
            src_ref=tiles.at[1],
            dst_ref=tiles.at[65],
            send_sem=halo_send.at[0],
            recv_sem=halo_recv.at[0],
            device_id=(vol - 1, me),
            device_id_type=MESH,
        )

    def downward():
        return pltpu.make_async_remote_copy(
            src_ref=tiles.at[64],
            dst_ref=tiles.at[0],
            send_sem=halo_send.at[1],
            recv_sem=halo_recv.at[1],
            device_id=(vol + 1, me),
            device_id_type=MESH,
        )

    @pl.when(vol > 0)
    def _():
        upward().start()

    @pl.when(vol < vols - 1)
    def _():
        downward().start()

    def give(target):
        pltpu.make_async_remote_copy(
            src_ref=tiles.at[pl.ds(target, 3)],
            dst_ref=got_ref.at[me],
            send_sem=send_sem,
            recv_sem=recv_sem.at[me],
            device_id=(vol, target),
            device_id_type=MESH,
        ).start()

    own = pltpu.make_async_copy(tiles.at[pl.ds(me, 3)], got_ref.at[me], recv_sem.at[me])
    at_edge = (me == 0) | (me == members - 1)

    @pl.when(jnp.logical_not(at_edge))
    def _():
        own.start()

    def targets(step):
        near = lax.rem(me - step + members, members)
        return near, lax.rem(near + HALF, members)

    def send_early(step, carry):
        for target in targets(step):
            @pl.when((target != 0) & (target != members - 1) & (target != me))
            def _():
                give(target)
        return carry

    def send_late(step, carry):
        for target in targets(step):
            give(target)
        return carry

    lax.fori_loop(0, EARLY, send_early, 0)

    @pl.when(vol < vols - 1)
    def _():
        upward().wait_recv()

    @pl.when(vol > 0)
    def _():
        downward().wait_recv()

    @pl.when(at_edge)
    def _():
        own.start()

    for target in (0, members - 1):
        @pl.when((lax.rem(me - target + members, HALF) < EARLY) & (me != target))
        def _():
            give(target)

    lax.fori_loop(EARLY, HALF, send_late, 0)

    def arrive(turn):
        @pl.when(turn < HALF // 2)
        def _():
            for half in range(2):
                for shift in (0, HALF):
                    z = lax.rem(me + 2 * turn + half + shift, DEPTH)
                    pltpu.make_async_copy(got_ref.at[z], got_ref.at[z], recv_sem.at[z]).wait()

    convolve_slices(me, arrive, got_ref, laid, held, out_ref)

    @pl.when(vol > 0)
    def _():
        upward().wait_send()

    @pl.when(vol < vols - 1)
    def _():
        downward().wait_send()

    rest = got_ref.at[pl.ds(0, 63)]
    pltpu.make_async_copy(rest, rest, send_sem).wait()


def encode(volume, *raw):
    fetched = (*raw, *tables())
    return pl.pallas_call(
        encoder_kernel,
        out_shape=jax.ShapeDtypeStruct((DEPTH, 48, 128), BF16),
        in_specs=[pl.BlockSpec(memory_space=pltpu.HBM)] * 19,
        out_specs=pl.BlockSpec(memory_space=pltpu.VMEM),
        scratch_shapes=[
            pltpu.VMEM(volume.shape, BF16),
            *[pltpu.VMEM(value.shape, value.dtype) for value in fetched],
            pltpu.VMEM((256, 72), BF16),
            pltpu.VMEM((256, 128), F32),
            pltpu.VMEM((192, 512), BF16),
            pltpu.VMEM((192, 128), F32),
            pltpu.VMEM((96, 192), BF16),
            pltpu.VMEM((96, 128), F32),
            pltpu.VMEM((144, 288), BF16),
            pltpu.VMEM((48, 128), F32),
            pltpu.VMEM((HALF // 2, 2, 48, 256), F32),
            pltpu.VMEM((2, 512, 256), BF16),
            pltpu.VMEM((2, 192, 256), BF16),
            pltpu.VMEM((2, 288, 256), BF16),
            pltpu.VMEM((66, 8, 128), BF16),
            pltpu.VMEM((DEPTH, 3, 8, 128), BF16),
            pltpu.SemaphoreType.DMA((19,)),
            pltpu.SemaphoreType.DMA((2,)),
            pltpu.SemaphoreType.DMA((2,)),
            pltpu.SemaphoreType.DMA,
            pltpu.SemaphoreType.DMA((DEPTH,)),
        ],
        compiler_params=pltpu.CompilerParams(
            collective_id=0, has_side_effects=True, vmem_limit_bytes=56 * 1024 * 1024
        ),
        name="encode",
    )(volume, *fetched)


def shards(volume, w1, o1, w2, o2, w3, o3, w4, o4):
    done = encode(
        volume,
        w1,
        o1[None],
        w2,
        o2[None],
        w3.transpose(1, 0, 2),
        o3[None],
        w4.transpose(1, 2, 0),
        o4[None],
    )
    return done.reshape(DEPTH, 24, 2, 128)


def solution(mesh):
    return jax.shard_map(
        shards,
        mesh=mesh,
        in_specs=(P("zs", "vol", None), P(), P(), P(), P(), P(), P(), P(), P()),
        out_specs=P(None, None, ("vol", "zs"), None),
        check_vma=False,
    )
```

```python
import functools

import jax
import jax.numpy as jnp
import numpy as np
from jax import lax
from jax.experimental import pallas as pl
from jax.experimental.pallas import tpu as pltpu
from jax.sharding import PartitionSpec as P

BF16 = jnp.bfloat16
F32 = jnp.float32
MESH = pl.DeviceIdType.MESH
DEPTH = 64
HALF = DEPTH // 2


def tables():
    place1 = np.zeros((3, 256, 12), np.float32)
    mask1 = np.zeros((256, 180), np.float32)
    pick1 = np.zeros((180, 9), np.float32)
    lay1 = np.zeros((180, 80), np.float32)
    source = ({0: (0, 1), 1: (1, 0), 2: (1, 1)}, {0: (1, 0), 1: (1, 1), 2: (2, 0)})
    for parity in range(2):
        for row in range(10):
            kind = parity * 10 + row
            for chan in range(12):
                at = parity * 128 + chan * 10 + row
                place1[0, at, chan] = 1
                place1[1, at, chan] = row >= 3
                place1[2, at, chan] = row < 7
                mask1[at, kind * 9 : kind * 9 + 9] = 1
            for along_x in range(3):
                for along_y in range(3):
                    tap = 3 * along_x + along_y
                    pick1[kind * 9 + tap, tap] = 1
                    shift, origin = source[parity][along_y]
                    fine = row + along_x
                    column = shift * 24 + (fine // 4) * 8 + origin * 4 + fine % 4
                    lay1[kind * 9 + tap, column] = 1
    place2 = np.zeros((96, 12), np.float32)
    lay2 = np.zeros((9, 12, 1024), np.float32)
    block = ({0: 0, 1: 1, 2: 2}, {0: 1, 1: 2, 2: 3})
    for chan in range(12):
        place2[chan * 8 : chan * 8 + 8, chan] = 1
        for along_x in range(3):
            for along_y in range(3):
                for parity in range(2):
                    column = parity * 512 + block[parity][along_y] * 128 + chan * 10 + along_x
                    lay2[3 * along_x + along_y, chan, column] = 1
    place3 = np.zeros((3, 96, 24), np.float32)
    for chan in range(24):
        for row in range(4):
            place3[0, chan * 4 + row, chan] = 1
            place3[1, chan * 4 + row, chan] = row >= 1
            place3[2, chan * 4 + row, chan] = row < 3
    lay3 = np.zeros((12, 4, 256), np.float32)
    for a in range(2):
        for b in range(2):
            for chan in range(12):
                lay3[chan, 2 * a + b, b * 96 + chan * 8 + a] = 1
    place4 = np.zeros((48, 24), np.float32)
    lay4 = np.zeros((24, 27, 1152), np.float32)
    for chan in range(24):
        place4[chan * 2 : chan * 2 + 2, chan] = 1
        for along_z in range(3):
            for along_x in range(3):
                for along_y in range(3):
                    tap = 9 * along_z + 3 * along_x + along_y
                    lay4[chan, tap, along_z * 384 + along_y * 96 + chan * 4 + along_x] = 1
    made = (place1, mask1, pick1, lay1, place2, lay2, place3, lay3, place4, lay4)
    return [table.astype(jnp.bfloat16) for table in made]


def mul(a, b):
    return jnp.dot(a, b, preferred_element_type=F32)


def mul_t(a, b):
    return lax.dot_general(a, b, (((1,), (1,)), ((), ())), preferred_element_type=F32)


def column(place, offset):
    return jnp.sum(place.astype(F32) * offset, axis=1, keepdims=True)


def with_bias(weight, bias, start):
    high = bias.astype(BF16).astype(F32)
    middle = (bias - high).astype(BF16).astype(F32)
    low = bias - high - middle
    lane = lax.broadcasted_iota(jnp.int32, weight.shape, 1)
    for shift, part in enumerate((high, middle, low)):
        weight = jnp.where(lane == start + shift, part, weight)
    return weight.astype(BF16)


def lay_weights(edge, raw, consts, laid):
    w1_ref, o1_ref, w2_ref, o2_ref, w3_ref, o3_ref, w4_ref, o4_ref = raw
    place1, mask1, pick1, lay1, place2, lay2, place3, lay3, place4, lay4 = consts
    m1, m2, m3, b3, m4 = laid

    here1, here2, here3 = place1[edge], place2[...], place3[edge]
    taps1 = mul(pick1[...], w1_ref[...]).astype(BF16)
    taps2 = [mul_t(here2, w2_ref[tap]).astype(BF16) for tap in range(9)]
    taps3 = [mul_t(here3, w3_ref[chan]).astype(BF16) for chan in range(12)]
    wide4 = sum(mul(w4_ref[chan], lay4[chan]) for chan in range(24)).astype(BF16)

    chosen = mul_t(here1, taps1) * mask1[...].astype(F32)
    base2 = sum(mul(taps2[tap], lay2[tap]) for tap in range(9))
    base3 = sum(mul(taps3[chan], lay3[chan]) for chan in range(12))
    base4 = mul(place4[...], wide4)

    row = lax.broadcasted_iota(jnp.int32, (256, 1), 0) & 127
    bias1 = jnp.where(row >= 120, 1.0, column(here1, o1_ref[...]))
    m1[...] = with_bias(mul(chosen.astype(BF16), lay1[...]), bias1, 72)
    bias2 = column(here2, o2_ref[...])
    for parity in range(2):
        for block in range(4):
            start = parity * 512 + block * 128
            rows = [
                pltpu.roll(base2[8 * c : 8 * c + 8, start : start + 128], 0, 1, stride=1, stride_axis=0)
                for c in range(12)
            ]
            placed = jnp.concatenate(rows, axis=0)
            placed = with_bias(placed, bias2, 120) if block == 1 else placed.astype(BF16)
            m2[96 * parity : 96 * parity + 96, 128 * block : 128 * block + 128] = placed
    row = lax.broadcasted_iota(jnp.int32, base3.shape, 0) & 3
    placed = base3
    for r in range(1, 4):
        placed = jnp.where(row == r, pltpu.roll(base3, 2 * r, 1), placed)
    m3[...] = placed[:, :192].astype(BF16)
    row = lax.broadcasted_iota(jnp.int32, base4.shape, 0) & 1
    placed = jnp.where(row == 1, pltpu.roll(base4, 1, 1), base4)
    bias4 = column(place4[...], o4_ref[...])
    for dz in range(3):
        part = placed[:, 384 * dz : 384 * dz + 304]
        part = with_bias(part, bias4, 288) if dz == 1 else part.astype(BF16)
        m4[48 * dz : 48 * dz + 48] = part
    b3[...] = jnp.broadcast_to(column(here3, o3_ref[...]), (96, 128))


def from_left(value, lane):
    return jnp.where(lane == 0, jnp.zeros((), BF16), pltpu.roll(value, 1, 1))


def from_right(value, lane):
    return jnp.where(lane == 127, jnp.zeros((), BF16), pltpu.roll(value, 127, 1))


def both(function, value):
    lane = lax.broadcasted_iota(jnp.int32, (value.shape[0], 128), 1)
    return jnp.concatenate([function(value[:, :128], lane), function(value[:, 128:], lane)], axis=1)


def twice(bias):
    return jnp.concatenate([bias, bias], axis=1)


def relu(value):
    return jnp.maximum(value.astype(BF16), jnp.zeros((), BF16))


def swap(value):
    return jnp.concatenate([value[:, 128:], value[:, :128]], axis=1)


def place_first(x_ref, m1, first_ref, lows):
    for half, (low, high) in enumerate(lows):
        field = jnp.concatenate(
            [x_ref[low].astype(F32).reshape(24, 128), x_ref[high].astype(F32).reshape(24, 128)], axis=1
        )
        lane = lax.broadcasted_iota(jnp.int32, field.shape, 1) & 127
        before = jnp.concatenate(
            [pltpu.roll(field[:, :128], 1, 1), pltpu.roll(field[:, 128:], 1, 1)], axis=1
        )
        after = jnp.concatenate(
            [pltpu.roll(field[:, :128], 127, 1), pltpu.roll(field[:, 128:], 127, 1)], axis=1
        )
        before = jnp.where(lane == 0, 0.0, before)
        after = jnp.where(lane == 127, 0.0, after)
        stacked = jnp.concatenate([before, field, after, jnp.ones((8, 256), F32)], axis=0)
        first = relu(mul(m1[...], stacked.astype(BF16)))
        even, odd = first[:128], first[128:]
        first_ref[half, :128] = both(from_left, odd)
        first_ref[half, 128:256] = even
        first_ref[half, 256:384] = odd
        first_ref[half, 384:] = both(from_right, even)


def place_second(first_ref, m2, second_ref):
    for half in range(2):
        second_ref[half] = relu(mul(m2[...], first_ref[half]))


def place_coarse(second_ref, m3, b3, coarse_ref):
    for half in range(2):
        coarse = relu(mul(m3[...], second_ref[half]) + twice(b3[...]))
        coarse_ref[half, :96] = both(from_left, coarse)
        coarse_ref[half, 96:192] = coarse
        coarse_ref[half, 192:288] = both(from_right, coarse)


def convolve_slices(me, arrive, leave, x_ref, laid, held, out_ref):
    m1, m2, m3, b3, m4 = laid
    first_ref, second_ref, coarse_ref = held
    coarse_ref[:, 288:] = jnp.ones((2, 16, 256), BF16)
    groups = HALF // 2

    def up(step):
        return lax.rem(me + step, DEPTH)

    def down(step):
        return lax.rem(me - 1 - step + 2 * DEPTH, DEPTH)

    def stage1(turn):
        pairs = [(up(2 * turn + half), down(2 * turn + half)) for half in range(2)]
        place_first(x_ref, m1, first_ref, pairs)

    def stage2():
        place_second(first_ref, m2, second_ref)

    def stage3():
        place_coarse(second_ref, m3, b3, coarse_ref)

    def joined(step, part):
        low = jnp.where(up(step) == 0, 0.0, part[:, :128])
        return jnp.concatenate([low, jnp.where(down(step) == DEPTH - 1, 0.0, part[:, 128:])], axis=1)

    def emit(step, total):
        done = relu(total)
        out_ref[up(step)] = done[:, :128]
        out_ref[down(step)] = done[:, 128:]
        leave(up(step))
        leave(down(step))

    def stage4(group, carry):
        for half in range(2):
            step = 2 * group + half
            deep = mul(m4[...], coarse_ref[half])
            here = deep[48:96]
            back = jnp.concatenate([deep[96:, :128], deep[:48, 128:]], axis=1)
            forth = jnp.concatenate([deep[:48, :128], deep[96:, 128:]], axis=1)
            if carry is None:
                carry = here + jnp.where(me == 0, 0.0, swap(back)), forth
            else:
                closing, opening = carry
                emit(step - 1, closing + joined(step, back))
                carry = here + joined(step, opening), forth
        return carry

    arrive(0)
    stage1(0)
    arrive(1)
    stage2()
    stage1(1)
    arrive(2)
    stage3()
    stage2()
    stage1(2)
    arrive(3)
    carry = stage4(0, None)
    stage3()
    stage2()
    stage1(3)

    def step(turn, carry):
        for more in range(2):
            arrive(4 + 2 * turn + more)
        for more in range(2):
            carry = stage4(1 + 2 * turn + more, carry)
            stage3()
            stage2()
            stage1(4 + 2 * turn + more)
        return carry

    carry = lax.fori_loop(0, (groups - 4) // 2, step, carry)
    carry = stage4(groups - 3, carry)
    stage3()
    stage2()
    carry = stage4(groups - 2, carry)
    stage3()
    closing, opening = stage4(groups - 1, carry)
    emit(HALF - 1, closing + jnp.where(me == HALF, 0.0, swap(opening)))


def encoder_kernel(*refs):
    volume_hbm, fetched_hbm, out_hbm = refs[0], refs[1:19], refs[19]
    volume_ref, fetched = refs[20], refs[21:39]
    laid, held = refs[39:44], refs[44:47]
    tiles, got_ref, out_ref = refs[47:50]
    fetch_sem, edge_sem, send_sem, out_sem, recv_sem = refs[50:]
    vol, me = lax.axis_index("vol"), lax.axis_index("zs")
    vols, members = lax.axis_size("vol"), lax.axis_size("zs")
    has_before, has_after = vol > 0, vol < vols - 1
    at_first, at_last = me == 0, me == members - 1

    load = pltpu.make_async_copy(volume_hbm, volume_ref, fetch_sem.at[18])
    load.start()
    loads = [
        pltpu.make_async_copy(source, target, fetch_sem.at[at])
        for at, (source, target) in enumerate(zip(fetched_hbm, fetched))
    ]
    barrier = pltpu.get_barrier_semaphore()

    def signal(vol_index, member):
        pl.semaphore_signal(barrier, inc=1, device_id=(vol_index, member), device_id_type=MESH)

    def greet(step, carry):
        signal(vol, lax.rem(me + step, members))
        return carry

    def greet_before(member, carry):
        signal(vol - 1, member)
        return carry

    def greet_after(member, carry):
        signal(vol + 1, member)
        return carry

    lax.fori_loop(1, members, greet, 0, unroll=9)

    @pl.when(has_before & at_first)
    def _():
        lax.fori_loop(0, members, greet_before, 0, unroll=8)

    @pl.when(has_after & at_last)
    def _():
        lax.fori_loop(0, members, greet_after, 0, unroll=8)

    for each in loads:
        each.start()
    load.wait()

    line = lax.broadcasted_iota(jnp.int32, (256, 256), 0)
    lane = lax.broadcasted_iota(jnp.int32, (256, 256), 1)
    parted = (line == jnp.where(lane < 128, 2 * lane, 2 * lane - 255)).astype(F32).astype(BF16)
    split = mul(volume_ref[0], parted)
    even = split[:, :128].reshape(32, 8, 128)
    odd = split[:, 128:].reshape(32, 8, 128)
    row = lax.broadcasted_iota(jnp.int32, (32, 8, 128), 1)
    upper = jnp.where(row < 4, even, pltpu.roll(odd, 4, 1))
    lower = jnp.where(row < 4, pltpu.roll(even, 4, 1), odd)
    tiles[1:65] = jnp.stack([upper, lower], axis=1).reshape(64, 8, 128).astype(BF16)

    tiles[0] = jnp.zeros((8, 128), BF16)
    tiles[65] = jnp.zeros((8, 128), BF16)

    pl.semaphore_wait(
        barrier, members - 1 + jnp.where(has_before, 1, 0) + jnp.where(has_after, 1, 0)
    )

    def give(start, count, slot, to, sem):
        return pltpu.make_async_remote_copy(
            src_ref=tiles.at[pl.ds(start, count)],
            dst_ref=got_ref.at[me, pl.ds(slot, count)],
            send_sem=sem,
            recv_sem=recv_sem.at[me],
            device_id=to,
            device_id_type=MESH,
        )

    edges = (
        (has_before & jnp.logical_not(at_first), give(1, 2, 1, (vol, 0), edge_sem.at[0])),
        (has_before, give(1, 1, 2, (vol - 1, members - 1), edge_sem.at[1])),
        (has_after & jnp.logical_not(at_last), give(63, 2, 0, (vol, members - 1), edge_sem.at[2])),
        (has_after, give(64, 1, 0, (vol + 1, 0), edge_sem.at[3])),
    )
    for wanted, copy in edges:
        pl.when(wanted)(copy.start)

    def send(step, carry):
        for target in (lax.rem(me - step + members, members), lax.rem(me + 1 + step, members)):
            partial = (has_before & (target == 0)) | (has_after & (target == members - 1))

            @pl.when(jnp.logical_not(partial) & (target != me))
            def _():
                give(target, 3, 0, (vol, target), send_sem).start()

        return carry

    lax.fori_loop(0, HALF, send, 0, unroll=4)

    def keep(start, count, slot):
        pltpu.make_async_copy(
            tiles.at[pl.ds(start, count)], got_ref.at[me, pl.ds(slot, count)], recv_sem.at[me]
        ).start()

    keep_first, keep_last = has_before & at_first, has_after & at_last
    pl.when(keep_first)(lambda: keep(1, 2, 1))
    pl.when(keep_last)(lambda: keep(63, 2, 0))
    pl.when(jnp.logical_not(keep_first | keep_last))(lambda: keep(me, 3, 0))

    for each in loads:
        each.wait()
    edge = jnp.where(
        (vol == 0) & at_first, 1, jnp.where((vol == vols - 1) & at_last, 2, 0)
    )
    lay_weights(edge, fetched[:8], fetched[8:], laid)

    def arrive(turn):
        for half in range(2):
            step = 2 * turn + half
            for z in (lax.rem(me + step, members), lax.rem(me - 1 - step + 2 * members, members)):
                pltpu.make_async_copy(got_ref.at[z], got_ref.at[z], recv_sem.at[z]).wait()

    def leave(slot):
        pltpu.make_async_copy(out_ref.at[slot], out_hbm.at[slot], out_sem).start()

    convolve_slices(me, arrive, leave, got_ref, laid, held, out_ref)

    for wanted, copy in edges:
        pl.when(wanted)(copy.wait_send)
    partials = jnp.where(edges[0][0], 1, 0) + jnp.where(edges[2][0], 1, 0)
    for count in range(3):
        @pl.when(partials == count)
        def _():
            rest = got_ref.at[pl.ds(0, 63 - count)]
            pltpu.make_async_copy(rest, rest, send_sem).wait()
    pltpu.make_async_copy(out_ref, out_hbm, out_sem).wait()


def encode(volume, *raw):
    fetched = (*raw, *tables())
    return pl.pallas_call(
        encoder_kernel,
        out_shape=jax.ShapeDtypeStruct((DEPTH, 48, 128), BF16),
        in_specs=[pl.BlockSpec(memory_space=pltpu.HBM)] * 19,
        out_specs=pl.BlockSpec(memory_space=pltpu.HBM),
        scratch_shapes=[
            pltpu.VMEM(volume.shape, BF16),
            *[pltpu.VMEM(value.shape, value.dtype) for value in fetched],
            pltpu.VMEM((256, 80), BF16),
            pltpu.VMEM((192, 512), BF16),
            pltpu.VMEM((96, 192), BF16),
            pltpu.VMEM((96, 128), F32),
            pltpu.VMEM((144, 304), BF16),
            pltpu.VMEM((2, 512, 256), BF16),
            pltpu.VMEM((2, 192, 256), BF16),
            pltpu.VMEM((2, 304, 256), BF16),
            pltpu.VMEM((66, 8, 128), BF16),
            pltpu.VMEM((DEPTH, 3, 8, 128), BF16),
            pltpu.VMEM((DEPTH, 48, 128), BF16),
            pltpu.SemaphoreType.DMA((19,)),
            pltpu.SemaphoreType.DMA((4,)),
            pltpu.SemaphoreType.DMA,
            pltpu.SemaphoreType.DMA,
            pltpu.SemaphoreType.DMA((DEPTH,)),
        ],
        compiler_params=pltpu.CompilerParams(
            collective_id=0, has_side_effects=True, vmem_limit_bytes=56 * 1024 * 1024
        ),
        name="encode",
    )(volume, *fetched)


CHUNKS = 8


def hand_kernel(source, target, held, in_sem, out_sem):
    rows = DEPTH // CHUNKS
    parts = [pl.ds(at * rows, rows) for at in range(CHUNKS)]
    into = [
        pltpu.make_async_copy(source.at[part], held.at[part], in_sem.at[at])
        for at, part in enumerate(parts)
    ]
    out = [
        pltpu.make_async_copy(held.at[part], target.at[part], out_sem.at[at])
        for at, part in enumerate(parts)
    ]
    for copy in into:
        copy.start()
    for first, second in zip(into, out):
        first.wait()
        second.start()
    for copy in out:
        copy.wait()


def hand(done):
    return pl.pallas_call(
        hand_kernel,
        out_shape=jax.ShapeDtypeStruct(done.shape, BF16),
        in_specs=[pl.BlockSpec(memory_space=pltpu.HBM)],
        out_specs=pl.BlockSpec(memory_space=pltpu.HBM),
        scratch_shapes=[
            pltpu.VMEM(done.shape, BF16),
            pltpu.SemaphoreType.DMA((CHUNKS,)),
            pltpu.SemaphoreType.DMA((CHUNKS,)),
        ],
        compiler_params=pltpu.CompilerParams(vmem_limit_bytes=56 * 1024 * 1024),
        name="hand",
    )(done)


def shards(volume, w1, o1, w2, o2, w3, o3, w4, o4):
    done = encode(
        volume,
        w1,
        o1[None],
        w2,
        o2[None],
        w3.transpose(1, 0, 2),
        o3[None],
        w4.transpose(1, 2, 0),
        o4[None],
    )
    return hand(done).reshape(DEPTH, 24, 2, 128)


def solution(mesh):
    return jax.shard_map(
        shards,
        mesh=mesh,
        in_specs=(P("zs", "vol", None), P(), P(), P(), P(), P(), P(), P(), P()),
        out_specs=P(None, None, ("vol", "zs"), None),
        check_vma=False,
    )
```

```python
import functools

import jax
import jax.numpy as jnp
import numpy as np
from jax import lax
from jax.experimental import pallas as pl
from jax.experimental.pallas import tpu as pltpu
from jax.sharding import PartitionSpec as P

BF16 = jnp.bfloat16
F32 = jnp.float32
MESH = pl.DeviceIdType.MESH
DEPTH = 64
HALF = DEPTH // 2


def tables():
    place1 = np.zeros((3, 256, 12), np.float32)
    mask1 = np.zeros((256, 180), np.float32)
    pick1 = np.zeros((180, 9), np.float32)
    lay1 = np.zeros((180, 80), np.float32)
    source = ({0: (0, 1), 1: (1, 0), 2: (1, 1)}, {0: (1, 0), 1: (1, 1), 2: (2, 0)})
    for parity in range(2):
        for row in range(10):
            kind = parity * 10 + row
            for chan in range(12):
                at = parity * 128 + chan * 10 + row
                place1[0, at, chan] = 1
                place1[1, at, chan] = row >= 3
                place1[2, at, chan] = row < 7
                mask1[at, kind * 9 : kind * 9 + 9] = 1
            for along_x in range(3):
                for along_y in range(3):
                    tap = 3 * along_x + along_y
                    pick1[kind * 9 + tap, tap] = 1
                    shift, origin = source[parity][along_y]
                    fine = row + along_x
                    column = shift * 24 + (fine // 4) * 8 + origin * 4 + fine % 4
                    lay1[kind * 9 + tap, column] = 1
    place2 = np.zeros((96, 12), np.float32)
    lay2 = np.zeros((9, 12, 1024), np.float32)
    block = ({0: 0, 1: 1, 2: 2}, {0: 1, 1: 2, 2: 3})
    for chan in range(12):
        place2[chan * 8 : chan * 8 + 8, chan] = 1
        for along_x in range(3):
            for along_y in range(3):
                for parity in range(2):
                    column = parity * 512 + block[parity][along_y] * 128 + chan * 10 + along_x
                    lay2[3 * along_x + along_y, chan, column] = 1
    place3 = np.zeros((3, 96, 24), np.float32)
    for chan in range(24):
        for row in range(4):
            place3[0, chan * 4 + row, chan] = 1
            place3[1, chan * 4 + row, chan] = row >= 1
            place3[2, chan * 4 + row, chan] = row < 3
    lay3 = np.zeros((12, 4, 256), np.float32)
    for a in range(2):
        for b in range(2):
            for chan in range(12):
                lay3[chan, 2 * a + b, b * 96 + chan * 8 + a] = 1
    place4 = np.zeros((48, 24), np.float32)
    lay4 = np.zeros((24, 27, 1152), np.float32)
    for chan in range(24):
        place4[chan * 2 : chan * 2 + 2, chan] = 1
        for along_z in range(3):
            for along_x in range(3):
                for along_y in range(3):
                    tap = 9 * along_z + 3 * along_x + along_y
                    lay4[chan, tap, along_z * 384 + along_y * 96 + chan * 4 + along_x] = 1
    made = (place1, mask1, pick1, lay1, place2, lay2, place3, lay3, place4, lay4)
    return [table.astype(jnp.bfloat16) for table in made]


def mul(a, b):
    return jnp.dot(a, b, preferred_element_type=F32)


def mul_t(a, b):
    return lax.dot_general(a, b, (((1,), (1,)), ((), ())), preferred_element_type=F32)


def column(place, offset):
    return jnp.sum(place.astype(F32) * offset, axis=1, keepdims=True)


def with_bias(weight, bias, start):
    high = bias.astype(BF16).astype(F32)
    middle = (bias - high).astype(BF16).astype(F32)
    low = bias - high - middle
    lane = lax.broadcasted_iota(jnp.int32, weight.shape, 1)
    for shift, part in enumerate((high, middle, low)):
        weight = jnp.where(lane == start + shift, part, weight)
    return weight.astype(BF16)


def lay_weights(edge, raw, consts, laid):
    w1_ref, o1_ref, w2_ref, o2_ref, w3_ref, o3_ref, w4_ref, o4_ref = raw
    place1, mask1, pick1, lay1, place2, lay2, place3, lay3, place4, lay4 = consts
    m1, m2, m3, b3, m4 = laid

    here1, here2, here3 = place1[edge], place2[...], place3[edge]
    taps1 = mul(pick1[...], w1_ref[...]).astype(BF16)
    taps2 = [mul_t(here2, w2_ref[tap]).astype(BF16) for tap in range(9)]
    taps3 = [mul_t(here3, w3_ref[chan]).astype(BF16) for chan in range(12)]
    wide4 = sum(mul(w4_ref[chan], lay4[chan]) for chan in range(24)).astype(BF16)

    chosen = mul_t(here1, taps1) * mask1[...].astype(F32)
    base2 = sum(mul(taps2[tap], lay2[tap]) for tap in range(9))
    base3 = sum(mul(taps3[chan], lay3[chan]) for chan in range(12))
    base4 = mul(place4[...], wide4)

    row = lax.broadcasted_iota(jnp.int32, (256, 1), 0) & 127
    bias1 = jnp.where(row >= 120, 1.0, column(here1, o1_ref[...]))
    m1[...] = with_bias(mul(chosen.astype(BF16), lay1[...]), bias1, 72)
    bias2 = column(here2, o2_ref[...])
    for parity in range(2):
        for block in range(4):
            start = parity * 512 + block * 128
            rows = [
                pltpu.roll(base2[8 * c : 8 * c + 8, start : start + 128], 0, 1, stride=1, stride_axis=0)
                for c in range(12)
            ]
            placed = jnp.concatenate(rows, axis=0)
            placed = with_bias(placed, bias2, 120) if block == 1 else placed.astype(BF16)
            m2[96 * parity : 96 * parity + 96, 128 * block : 128 * block + 128] = placed
    row = lax.broadcasted_iota(jnp.int32, base3.shape, 0) & 3
    placed = base3
    for r in range(1, 4):
        placed = jnp.where(row == r, pltpu.roll(base3, 2 * r, 1), placed)
    m3[...] = placed[:, :192].astype(BF16)
    row = lax.broadcasted_iota(jnp.int32, base4.shape, 0) & 1
    placed = jnp.where(row == 1, pltpu.roll(base4, 1, 1), base4)
    bias4 = column(place4[...], o4_ref[...])
    for dz in range(3):
        part = placed[:, 384 * dz : 384 * dz + 304]
        part = with_bias(part, bias4, 288) if dz == 1 else part.astype(BF16)
        m4[48 * dz : 48 * dz + 48] = part
    b3[...] = jnp.broadcast_to(column(here3, o3_ref[...]), (96, 128))


def from_left(value, lane):
    return jnp.where(lane == 0, jnp.zeros((), BF16), pltpu.roll(value, 1, 1))


def from_right(value, lane):
    return jnp.where(lane == 127, jnp.zeros((), BF16), pltpu.roll(value, 127, 1))


def both(function, value):
    lane = lax.broadcasted_iota(jnp.int32, (value.shape[0], 128), 1)
    return jnp.concatenate([function(value[:, :128], lane), function(value[:, 128:], lane)], axis=1)


def twice(bias):
    return jnp.concatenate([bias, bias], axis=1)


def relu(value):
    return jnp.maximum(value.astype(BF16), jnp.zeros((), BF16))


def swap(value):
    return jnp.concatenate([value[:, 128:], value[:, :128]], axis=1)


def place_first(x_ref, m1, first_ref, lows, spot):
    for half, (low, high) in enumerate(lows):
        field = jnp.concatenate(
            [x_ref[low].astype(F32).reshape(24, 128), x_ref[high].astype(F32).reshape(24, 128)], axis=1
        )
        lane = lax.broadcasted_iota(jnp.int32, field.shape, 1) & 127
        before = jnp.concatenate(
            [pltpu.roll(field[:, :128], 1, 1), pltpu.roll(field[:, 128:], 1, 1)], axis=1
        )
        after = jnp.concatenate(
            [pltpu.roll(field[:, :128], 127, 1), pltpu.roll(field[:, 128:], 127, 1)], axis=1
        )
        before = jnp.where(lane == 0, 0.0, before)
        after = jnp.where(lane == 127, 0.0, after)
        stacked = jnp.concatenate([before, field, after, jnp.ones((8, 256), F32)], axis=0)
        first = relu(mul(m1[...], stacked.astype(BF16)))
        even, odd = first[:128], first[128:]
        first_ref[spot + half, :128] = both(from_left, odd)
        first_ref[spot + half, 128:256] = even
        first_ref[spot + half, 256:384] = odd
        first_ref[spot + half, 384:] = both(from_right, even)


def place_second(first_ref, m2, second_ref, spot):
    for at in (spot, spot + 1):
        second_ref[at] = relu(mul(m2[...], first_ref[at]))


def place_coarse(second_ref, m3, b3, coarse_ref, spot):
    for at in (spot, spot + 1):
        coarse = relu(mul(m3[...], second_ref[at]) + twice(b3[...]))
        coarse_ref[at, :96] = both(from_left, coarse)
        coarse_ref[at, 96:192] = coarse
        coarse_ref[at, 192:288] = both(from_right, coarse)


def convolve_slices(me, arrive, leave, x_ref, laid, held, out_ref):
    m1, m2, m3, b3, m4 = laid
    first_ref, second_ref, coarse_ref = held
    coarse_ref[:, 288:] = jnp.ones((4, 16, 256), BF16)
    groups = HALF // 2

    def up(step):
        return lax.rem(me + step, DEPTH)

    def down(step):
        return lax.rem(me - 1 - step + 2 * DEPTH, DEPTH)

    def stage1(turn, odd):
        pairs = [(up(2 * turn + half), down(2 * turn + half)) for half in range(2)]
        place_first(x_ref, m1, first_ref, pairs, 2 * odd)

    def stage2(odd):
        place_second(first_ref, m2, second_ref, 2 * odd)

    def stage3(odd):
        place_coarse(second_ref, m3, b3, coarse_ref, 2 * odd)

    def joined(step, part):
        low = jnp.where(up(step) == 0, 0.0, part[:, :128])
        return jnp.concatenate([low, jnp.where(down(step) == DEPTH - 1, 0.0, part[:, 128:])], axis=1)

    def emit(step, total):
        done = relu(total)
        out_ref[up(step)] = done[:, :128]
        out_ref[down(step)] = done[:, 128:]
        leave(up(step))
        leave(down(step))

    def stage4(group, odd, carry):
        for half in range(2):
            step = 2 * group + half
            deep = mul(m4[...], coarse_ref[2 * odd + half])
            here = deep[48:96]
            back = jnp.concatenate([deep[96:, :128], deep[:48, 128:]], axis=1)
            forth = jnp.concatenate([deep[:48, :128], deep[96:, 128:]], axis=1)
            if carry is None:
                carry = here + jnp.where(me == 0, 0.0, swap(back)), forth
            else:
                closing, opening = carry
                emit(step - 1, closing + joined(step, back))
                carry = here + joined(step, opening), forth
        return carry

    arrive(0)
    stage1(0, 0)
    arrive(1)
    stage2(0)
    stage1(1, 1)
    arrive(2)
    stage3(0)
    stage2(1)
    stage1(2, 0)
    arrive(3)
    carry = stage4(0, 0, None)
    stage3(1)
    stage2(0)
    stage1(3, 1)

    def step(turn, carry):
        for more in range(2):
            arrive(4 + 2 * turn + more)
        for more in range(2):
            carry = stage4(1 + 2 * turn + more, 1 - more, carry)
            stage3(more)
            stage2(1 - more)
            stage1(4 + 2 * turn + more, more)
        return carry

    carry = lax.fori_loop(0, (groups - 6) // 2, step, carry)
    arrive(groups - 2)
    carry = stage4(groups - 5, 1, carry)
    stage3(0)
    stage2(1)
    stage1(groups - 2, 0)
    arrive(groups - 1)
    stage1(groups - 1, 1)
    carry = stage4(groups - 4, 0, carry)
    stage2(0)
    stage3(1)
    stage2(1)
    stage3(0)
    carry = stage4(groups - 3, 1, carry)
    stage3(1)
    carry = stage4(groups - 2, 0, carry)
    closing, opening = stage4(groups - 1, 1, carry)
    emit(HALF - 1, closing + jnp.where(me == HALF, 0.0, swap(opening)))


def encoder_kernel(*refs):
    volume_hbm, fetched_hbm, out_hbm = refs[0], refs[1:19], refs[19]
    volume_ref, fetched = refs[20], refs[21:39]
    laid, held = refs[39:44], refs[44:47]
    tiles, got_ref, out_ref = refs[47:50]
    fetch_sem, edge_sem, send_sem, out_sem, recv_sem = refs[50:]
    vol, me = lax.axis_index("vol"), lax.axis_index("zs")
    vols, members = lax.axis_size("vol"), lax.axis_size("zs")
    has_before, has_after = vol > 0, vol < vols - 1
    at_first, at_last = me == 0, me == members - 1

    load = pltpu.make_async_copy(volume_hbm, volume_ref, fetch_sem.at[18])
    load.start()
    loads = [
        pltpu.make_async_copy(source, target, fetch_sem.at[at])
        for at, (source, target) in enumerate(zip(fetched_hbm, fetched))
    ]
    barrier = pltpu.get_barrier_semaphore()

    def signal(vol_index, member):
        pl.semaphore_signal(barrier, inc=1, device_id=(vol_index, member), device_id_type=MESH)

    def greet(step, carry):
        signal(vol, lax.rem(me + step, members))
        return carry

    def greet_before(member, carry):
        signal(vol - 1, member)
        return carry

    def greet_after(member, carry):
        signal(vol + 1, member)
        return carry

    lax.fori_loop(1, members, greet, 0, unroll=9)

    @pl.when(has_before & at_first)
    def _():
        lax.fori_loop(0, members, greet_before, 0, unroll=8)

    @pl.when(has_after & at_last)
    def _():
        lax.fori_loop(0, members, greet_after, 0, unroll=8)

    for each in loads:
        each.start()
    load.wait()

    line = lax.broadcasted_iota(jnp.int32, (256, 256), 0)
    lane = lax.broadcasted_iota(jnp.int32, (256, 256), 1)
    parted = (line == jnp.where(lane < 128, 2 * lane, 2 * lane - 255)).astype(F32).astype(BF16)
    split = mul(volume_ref[0], parted)
    even = split[:, :128].reshape(32, 8, 128)
    odd = split[:, 128:].reshape(32, 8, 128)
    row = lax.broadcasted_iota(jnp.int32, (32, 8, 128), 1)
    upper = jnp.where(row < 4, even, pltpu.roll(odd, 4, 1))
    lower = jnp.where(row < 4, pltpu.roll(even, 4, 1), odd)
    tiles[1:65] = jnp.stack([upper, lower], axis=1).reshape(64, 8, 128).astype(BF16)

    tiles[0] = jnp.zeros((8, 128), BF16)
    tiles[65] = jnp.zeros((8, 128), BF16)

    pl.semaphore_wait(
        barrier, members - 1 + jnp.where(has_before, 1, 0) + jnp.where(has_after, 1, 0)
    )

    def give(start, count, slot, to, sem):
        return pltpu.make_async_remote_copy(
            src_ref=tiles.at[pl.ds(start, count)],
            dst_ref=got_ref.at[me, pl.ds(slot, count)],
            send_sem=sem,
            recv_sem=recv_sem.at[me],
            device_id=to,
            device_id_type=MESH,
        )

    edges = (
        (has_before & jnp.logical_not(at_first), give(1, 2, 1, (vol, 0), edge_sem.at[0])),
        (has_before, give(1, 1, 2, (vol - 1, members - 1), edge_sem.at[1])),
        (has_after & jnp.logical_not(at_last), give(63, 2, 0, (vol, members - 1), edge_sem.at[2])),
        (has_after, give(64, 1, 0, (vol + 1, 0), edge_sem.at[3])),
    )
    for wanted, copy in edges:
        pl.when(wanted)(copy.start)

    def send(step, carry):
        for target in (lax.rem(me - step + members, members), lax.rem(me + 1 + step, members)):
            partial = (has_before & (target == 0)) | (has_after & (target == members - 1))

            @pl.when(jnp.logical_not(partial) & (target != me))
            def _():
                give(target, 3, 0, (vol, target), send_sem).start()

        return carry

    lax.fori_loop(0, 8, send, 0, unroll=4)

    def keep(start, count, slot):
        pltpu.make_async_copy(
            tiles.at[pl.ds(start, count)], got_ref.at[me, pl.ds(slot, count)], recv_sem.at[me]
        ).start()

    keep_first, keep_last = has_before & at_first, has_after & at_last
    pl.when(keep_first)(lambda: keep(1, 2, 1))
    pl.when(keep_last)(lambda: keep(63, 2, 0))
    pl.when(jnp.logical_not(keep_first | keep_last))(lambda: keep(me, 3, 0))

    for each in loads:
        each.wait()
    edge = jnp.where(
        (vol == 0) & at_first, 1, jnp.where((vol == vols - 1) & at_last, 2, 0)
    )
    lay_weights(edge, fetched[:8], fetched[8:], laid)
    lax.fori_loop(8, 16, send, 0, unroll=4)

    def arrive(turn):
        if isinstance(turn, int) and 16 + 4 * turn < HALF:
            lax.fori_loop(16 + 4 * turn, 16 + 4 * (turn + 1), send, 0, unroll=4)
        for half in range(2):
            step = 2 * turn + half
            for z in (lax.rem(me + step, members), lax.rem(me - 1 - step + 2 * members, members)):
                pltpu.make_async_copy(got_ref.at[z], got_ref.at[z], recv_sem.at[z]).wait()

    def leave(slot):
        pltpu.make_async_copy(out_ref.at[slot], out_hbm.at[slot], out_sem).start()

    convolve_slices(me, arrive, leave, got_ref, laid, held, out_ref)

    for wanted, copy in edges:
        pl.when(wanted)(copy.wait_send)
    partials = jnp.where(edges[0][0], 1, 0) + jnp.where(edges[2][0], 1, 0)
    for count in range(3):
        @pl.when(partials == count)
        def _():
            rest = got_ref.at[pl.ds(0, 63 - count)]
            pltpu.make_async_copy(rest, rest, send_sem).wait()
    pltpu.make_async_copy(out_ref, out_hbm, out_sem).wait()


def encode(volume, *raw):
    fetched = (*raw, *tables())
    return pl.pallas_call(
        encoder_kernel,
        out_shape=jax.ShapeDtypeStruct((DEPTH, 48, 128), BF16),
        in_specs=[pl.BlockSpec(memory_space=pltpu.HBM)] * 19,
        out_specs=pl.BlockSpec(memory_space=pltpu.HBM),
        scratch_shapes=[
            pltpu.VMEM(volume.shape, BF16),
            *[pltpu.VMEM(value.shape, value.dtype) for value in fetched],
            pltpu.VMEM((256, 80), BF16),
            pltpu.VMEM((192, 512), BF16),
            pltpu.VMEM((96, 192), BF16),
            pltpu.VMEM((96, 128), F32),
            pltpu.VMEM((144, 304), BF16),
            pltpu.VMEM((4, 512, 256), BF16),
            pltpu.VMEM((4, 192, 256), BF16),
            pltpu.VMEM((4, 304, 256), BF16),
            pltpu.VMEM((66, 8, 128), BF16),
            pltpu.VMEM((DEPTH, 3, 8, 128), BF16),
            pltpu.VMEM((DEPTH, 48, 128), BF16),
            pltpu.SemaphoreType.DMA((19,)),
            pltpu.SemaphoreType.DMA((4,)),
            pltpu.SemaphoreType.DMA,
            pltpu.SemaphoreType.DMA,
            pltpu.SemaphoreType.DMA((DEPTH,)),
        ],
        compiler_params=pltpu.CompilerParams(
            collective_id=0, has_side_effects=True, vmem_limit_bytes=56 * 1024 * 1024
        ),
        name="encode",
    )(volume, *fetched)


CHUNKS = 4


def hand_kernel(source, target, held, in_sem, out_sem):
    rows = DEPTH // CHUNKS
    parts = [pl.ds(at * rows, rows) for at in range(CHUNKS)]
    into = [
        pltpu.make_async_copy(source.at[part], held.at[part], in_sem.at[at])
        for at, part in enumerate(parts)
    ]
    out = [
        pltpu.make_async_copy(held.at[part], target.at[part], out_sem.at[at])
        for at, part in enumerate(parts)
    ]
    for copy in into:
        copy.start()
    for first, second in zip(into, out):
        first.wait()
        second.start()
    for copy in out:
        copy.wait()


def hand(done):
    return pl.pallas_call(
        hand_kernel,
        out_shape=jax.ShapeDtypeStruct(done.shape, BF16),
        in_specs=[pl.BlockSpec(memory_space=pltpu.HBM)],
        out_specs=pl.BlockSpec(memory_space=pltpu.HBM),
        scratch_shapes=[
            pltpu.VMEM(done.shape, BF16),
            pltpu.SemaphoreType.DMA((CHUNKS,)),
            pltpu.SemaphoreType.DMA((CHUNKS,)),
        ],
        compiler_params=pltpu.CompilerParams(vmem_limit_bytes=56 * 1024 * 1024),
        name="hand",
    )(done)


def shards(volume, w1, o1, w2, o2, w3, o3, w4, o4):
    done = encode(
        volume,
        w1,
        o1[None],
        w2,
        o2[None],
        w3.transpose(1, 0, 2),
        o3[None],
        w4.transpose(1, 2, 0),
        o4[None],
    )
    return hand(done).reshape(DEPTH, 24, 2, 128)


def solution(mesh):
    return jax.shard_map(
        shards,
        mesh=mesh,
        in_specs=(P("zs", "vol", None), P(), P(), P(), P(), P(), P(), P(), P()),
        out_specs=P(None, None, ("vol", "zs"), None),
        check_vma=False,
    )
```

```python
import functools

import jax
import jax.numpy as jnp
import numpy as np
from jax import lax
from jax.experimental import pallas as pl
from jax.experimental.pallas import tpu as pltpu
from jax.sharding import PartitionSpec as P

BF16 = jnp.bfloat16
F32 = jnp.float32
MESH = pl.DeviceIdType.MESH
DEPTH = 64
HALF = DEPTH // 2


def tables():
    place1 = np.zeros((3, 256, 12), np.float32)
    mask1 = np.zeros((256, 180), np.float32)
    pick1 = np.zeros((180, 9), np.float32)
    lay1 = np.zeros((180, 80), np.float32)
    source = ({0: (0, 1), 1: (1, 0), 2: (1, 1)}, {0: (1, 0), 1: (1, 1), 2: (2, 0)})
    for parity in range(2):
        for row in range(10):
            kind = parity * 10 + row
            for chan in range(12):
                at = parity * 128 + chan * 10 + row
                place1[0, at, chan] = 1
                place1[1, at, chan] = row >= 3
                place1[2, at, chan] = row < 7
                mask1[at, kind * 9 : kind * 9 + 9] = 1
            for along_x in range(3):
                for along_y in range(3):
                    tap = 3 * along_x + along_y
                    pick1[kind * 9 + tap, tap] = 1
                    shift, origin = source[parity][along_y]
                    fine = row + along_x
                    column = shift * 24 + (fine // 4) * 8 + origin * 4 + fine % 4
                    lay1[kind * 9 + tap, column] = 1
    place2 = np.zeros((96, 12), np.float32)
    lay2 = np.zeros((9, 12, 1024), np.float32)
    block = ({0: 0, 1: 1, 2: 2}, {0: 1, 1: 2, 2: 3})
    for chan in range(12):
        place2[chan * 8 : chan * 8 + 8, chan] = 1
        for along_x in range(3):
            for along_y in range(3):
                for parity in range(2):
                    column = parity * 512 + block[parity][along_y] * 128 + chan * 10 + along_x
                    lay2[3 * along_x + along_y, chan, column] = 1
    place3 = np.zeros((3, 96, 24), np.float32)
    for chan in range(24):
        for row in range(4):
            place3[0, chan * 4 + row, chan] = 1
            place3[1, chan * 4 + row, chan] = row >= 1
            place3[2, chan * 4 + row, chan] = row < 3
    lay3 = np.zeros((12, 4, 256), np.float32)
    for a in range(2):
        for b in range(2):
            for chan in range(12):
                lay3[chan, 2 * a + b, b * 96 + chan * 8 + a] = 1
    place4 = np.zeros((48, 24), np.float32)
    lay4 = np.zeros((24, 27, 1152), np.float32)
    for chan in range(24):
        place4[chan * 2 : chan * 2 + 2, chan] = 1
        for along_z in range(3):
            for along_x in range(3):
                for along_y in range(3):
                    tap = 9 * along_z + 3 * along_x + along_y
                    lay4[chan, tap, along_z * 384 + along_y * 96 + chan * 4 + along_x] = 1
    made = (place1, mask1, pick1, lay1, place2, lay2, place3, lay3, place4, lay4)
    return [table.astype(jnp.bfloat16) for table in made]


def mul(a, b):
    return jnp.dot(a, b, preferred_element_type=F32)


def mul_t(a, b):
    return lax.dot_general(a, b, (((1,), (1,)), ((), ())), preferred_element_type=F32)


def column(place, offset):
    return jnp.sum(place.astype(F32) * offset, axis=1, keepdims=True)


def with_bias(weight, bias, start):
    high = bias.astype(BF16).astype(F32)
    middle = (bias - high).astype(BF16).astype(F32)
    low = bias - high - middle
    lane = lax.broadcasted_iota(jnp.int32, weight.shape, 1)
    for shift, part in enumerate((high, middle, low)):
        weight = jnp.where(lane == start + shift, part, weight)
    return weight.astype(BF16)


def lay_weights(edge, raw, consts, laid):
    w1_ref, o1_ref, w2_ref, o2_ref, w3_ref, o3_ref, w4_ref, o4_ref = raw
    place1, mask1, pick1, lay1, place2, lay2, place3, lay3, place4, lay4 = consts
    m1, m2, m3, b3, m4 = laid

    here1, here2, here3 = place1[edge], place2[...], place3[edge]
    taps1 = mul(pick1[...], w1_ref[...]).astype(BF16)
    taps2 = [mul_t(here2, w2_ref[tap]).astype(BF16) for tap in range(9)]
    taps3 = [mul_t(here3, w3_ref[chan]).astype(BF16) for chan in range(12)]
    wide4 = sum(mul(w4_ref[chan], lay4[chan]) for chan in range(24)).astype(BF16)

    chosen = mul_t(here1, taps1) * mask1[...].astype(F32)
    base2 = sum(mul(taps2[tap], lay2[tap]) for tap in range(9))
    base3 = sum(mul(taps3[chan], lay3[chan]) for chan in range(12))
    base4 = mul(place4[...], wide4)

    row = lax.broadcasted_iota(jnp.int32, (256, 1), 0) & 127
    bias1 = jnp.where(row >= 120, 1.0, column(here1, o1_ref[...]))
    m1[...] = with_bias(mul(chosen.astype(BF16), lay1[...]), bias1, 72)
    bias2 = column(here2, o2_ref[...])
    for parity in range(2):
        for block in range(4):
            start = parity * 512 + block * 128
            rows = [
                pltpu.roll(base2[8 * c : 8 * c + 8, start : start + 128], 0, 1, stride=1, stride_axis=0)
                for c in range(12)
            ]
            placed = jnp.concatenate(rows, axis=0)
            placed = with_bias(placed, bias2, 120) if block == 1 else placed.astype(BF16)
            m2[96 * parity : 96 * parity + 96, 128 * block : 128 * block + 128] = placed
    row = lax.broadcasted_iota(jnp.int32, base3.shape, 0) & 3
    placed = base3
    for r in range(1, 4):
        placed = jnp.where(row == r, pltpu.roll(base3, 2 * r, 1), placed)
    m3[...] = placed[:, :192].astype(BF16)
    row = lax.broadcasted_iota(jnp.int32, base4.shape, 0) & 1
    placed = jnp.where(row == 1, pltpu.roll(base4, 1, 1), base4)
    bias4 = column(place4[...], o4_ref[...])
    for dz in range(3):
        part = placed[:, 384 * dz : 384 * dz + 304]
        part = with_bias(part, bias4, 288) if dz == 1 else part.astype(BF16)
        m4[48 * dz : 48 * dz + 48] = part
    b3[...] = jnp.broadcast_to(column(here3, o3_ref[...]), (96, 128))


def from_left(value, lane):
    return jnp.where(lane == 0, jnp.zeros((), BF16), pltpu.roll(value, 1, 1))


def from_right(value, lane):
    return jnp.where(lane == 127, jnp.zeros((), BF16), pltpu.roll(value, 127, 1))


def both(function, value):
    lane = lax.broadcasted_iota(jnp.int32, (value.shape[0], 128), 1)
    return jnp.concatenate([function(value[:, :128], lane), function(value[:, 128:], lane)], axis=1)


def twice(bias):
    return jnp.concatenate([bias, bias], axis=1)


def relu(value):
    return jnp.maximum(value.astype(BF16), jnp.zeros((), BF16))


def swap(value):
    return jnp.concatenate([value[:, 128:], value[:, :128]], axis=1)


def place_first(x_ref, m1, first_ref, lows, spot):
    for half, (low, high) in enumerate(lows):
        field = jnp.concatenate(
            [x_ref[low].astype(F32).reshape(24, 128), x_ref[high].astype(F32).reshape(24, 128)], axis=1
        )
        lane = lax.broadcasted_iota(jnp.int32, field.shape, 1) & 127
        before = jnp.concatenate(
            [pltpu.roll(field[:, :128], 1, 1), pltpu.roll(field[:, 128:], 1, 1)], axis=1
        )
        after = jnp.concatenate(
            [pltpu.roll(field[:, :128], 127, 1), pltpu.roll(field[:, 128:], 127, 1)], axis=1
        )
        before = jnp.where(lane == 0, 0.0, before)
        after = jnp.where(lane == 127, 0.0, after)
        stacked = jnp.concatenate([before, field, after, jnp.ones((8, 256), F32)], axis=0)
        first = relu(mul(m1[...], stacked.astype(BF16)))
        even, odd = first[:128], first[128:]
        first_ref[spot + half, :128] = both(from_left, odd)
        first_ref[spot + half, 128:256] = even
        first_ref[spot + half, 256:384] = odd
        first_ref[spot + half, 384:] = both(from_right, even)


def place_second(first_ref, m2, second_ref, spot):
    for at in (spot, spot + 1):
        second_ref[at] = relu(mul(m2[...], first_ref[at]))


def place_coarse(second_ref, m3, b3, coarse_ref, spot):
    for at in (spot, spot + 1):
        coarse = relu(mul(m3[...], second_ref[at]) + twice(b3[...]))
        coarse_ref[at, :96] = both(from_left, coarse)
        coarse_ref[at, 96:192] = coarse
        coarse_ref[at, 192:288] = both(from_right, coarse)


def convolve_slices(me, arrive, leave, x_ref, laid, held, out_ref):
    m1, m2, m3, b3, m4 = laid
    first_ref, second_ref, coarse_ref = held
    coarse_ref[:, 288:] = jnp.ones((4, 16, 256), BF16)
    groups = HALF // 2

    def up(step):
        return lax.rem(me + step, DEPTH)

    def down(step):
        return lax.rem(me - 1 - step + 2 * DEPTH, DEPTH)

    def stage1(turn, odd):
        pairs = [(up(2 * turn + half), down(2 * turn + half)) for half in range(2)]
        place_first(x_ref, m1, first_ref, pairs, 2 * odd)

    def stage2(odd):
        place_second(first_ref, m2, second_ref, 2 * odd)

    def stage3(odd):
        place_coarse(second_ref, m3, b3, coarse_ref, 2 * odd)

    def joined(step, part):
        low = jnp.where(up(step) == 0, 0.0, part[:, :128])
        return jnp.concatenate([low, jnp.where(down(step) == DEPTH - 1, 0.0, part[:, 128:])], axis=1)

    def emit(step, total):
        done = relu(total)
        out_ref[up(step)] = done[:, :128]
        out_ref[down(step)] = done[:, 128:]
        leave(up(step))
        leave(down(step))

    def stage4(group, odd, carry):
        for half in range(2):
            step = 2 * group + half
            deep = mul(m4[...], coarse_ref[2 * odd + half])
            here = deep[48:96]
            back = jnp.concatenate([deep[96:, :128], deep[:48, 128:]], axis=1)
            forth = jnp.concatenate([deep[:48, :128], deep[96:, 128:]], axis=1)
            if carry is None:
                carry = here + jnp.where(me == 0, 0.0, swap(back)), forth
            else:
                closing, opening = carry
                emit(step - 1, closing + joined(step, back))
                carry = here + joined(step, opening), forth
        return carry

    arrive(0)
    stage1(0, 0)
    arrive(1)
    stage2(0)
    stage1(1, 1)
    arrive(2)
    stage3(0)
    stage2(1)
    stage1(2, 0)
    arrive(3)
    carry = stage4(0, 0, None)
    stage3(1)
    stage2(0)
    stage1(3, 1)

    def step(turn, carry):
        for more in range(2):
            arrive(4 + 2 * turn + more)
        for more in range(2):
            carry = stage4(1 + 2 * turn + more, 1 - more, carry)
            stage3(more)
            stage2(1 - more)
            stage1(4 + 2 * turn + more, more)
        return carry

    carry = lax.fori_loop(0, (groups - 6) // 2, step, carry)
    arrive(groups - 2)
    carry = stage4(groups - 5, 1, carry)
    stage3(0)
    stage2(1)
    stage1(groups - 2, 0)
    arrive(groups - 1)
    stage1(groups - 1, 1)
    carry = stage4(groups - 4, 0, carry)
    stage2(0)
    stage3(1)
    stage2(1)
    stage3(0)
    carry = stage4(groups - 3, 1, carry)
    stage3(1)
    carry = stage4(groups - 2, 0, carry)
    closing, opening = stage4(groups - 1, 1, carry)
    emit(HALF - 1, closing + jnp.where(me == HALF, 0.0, swap(opening)))


def encoder_kernel(*refs):
    volume_hbm, fetched_hbm, out_hbm = refs[0], refs[1:19], refs[19]
    volume_ref, fetched = refs[20], refs[21:39]
    laid, held = refs[39:44], refs[44:47]
    tiles, got_ref, out_ref = refs[47:50]
    fetch_sem, edge_sem, send_sem, out_sem, recv_sem = refs[50:]
    vol, me = lax.axis_index("vol"), lax.axis_index("zs")
    vols, members = lax.axis_size("vol"), lax.axis_size("zs")
    has_before, has_after = vol > 0, vol < vols - 1
    at_first, at_last = me == 0, me == members - 1

    load = pltpu.make_async_copy(volume_hbm, volume_ref, fetch_sem.at[18])
    load.start()
    loads = [
        pltpu.make_async_copy(source, target, fetch_sem.at[at])
        for at, (source, target) in enumerate(zip(fetched_hbm, fetched))
    ]
    barrier = pltpu.get_barrier_semaphore()

    def signal(vol_index, member):
        pl.semaphore_signal(barrier, inc=1, device_id=(vol_index, member), device_id_type=MESH)

    def greet(member, carry):
        pl.when(member != me)(lambda: signal(vol, member))
        return carry

    def greet_before(member, carry):
        signal(vol - 1, member)
        return carry

    def greet_after(member, carry):
        signal(vol + 1, member)
        return carry

    lax.fori_loop(0, members, greet, 0, unroll=8)

    @pl.when(has_before & at_first)
    def _():
        lax.fori_loop(0, members, greet_before, 0, unroll=8)

    @pl.when(has_after & at_last)
    def _():
        lax.fori_loop(0, members, greet_after, 0, unroll=8)

    for each in loads:
        each.start()
    load.wait()

    line = lax.broadcasted_iota(jnp.int32, (256, 256), 0)
    lane = lax.broadcasted_iota(jnp.int32, (256, 256), 1)
    parted = (line == jnp.where(lane < 128, 2 * lane, 2 * lane - 255)).astype(F32).astype(BF16)
    split = mul(volume_ref[0], parted)
    even = split[:, :128].reshape(32, 8, 128)
    odd = split[:, 128:].reshape(32, 8, 128)
    row = lax.broadcasted_iota(jnp.int32, (32, 8, 128), 1)
    upper = jnp.where(row < 4, even, pltpu.roll(odd, 4, 1))
    lower = jnp.where(row < 4, pltpu.roll(even, 4, 1), odd)
    tiles[1:65] = jnp.stack([upper, lower], axis=1).reshape(64, 8, 128).astype(BF16)

    tiles[0] = jnp.zeros((8, 128), BF16)
    tiles[65] = jnp.zeros((8, 128), BF16)

    pl.semaphore_wait(
        barrier, members - 1 + jnp.where(has_before, 1, 0) + jnp.where(has_after, 1, 0)
    )

    def give(start, count, slot, to, sem):
        return pltpu.make_async_remote_copy(
            src_ref=tiles.at[pl.ds(start, count)],
            dst_ref=got_ref.at[me, pl.ds(slot, count)],
            send_sem=sem,
            recv_sem=recv_sem.at[me],
            device_id=to,
            device_id_type=MESH,
        )

    edges = (
        (has_before & jnp.logical_not(at_first), give(1, 2, 1, (vol, 0), edge_sem.at[0])),
        (has_before, give(1, 1, 2, (vol - 1, members - 1), edge_sem.at[1])),
        (has_after & jnp.logical_not(at_last), give(63, 2, 0, (vol, members - 1), edge_sem.at[2])),
        (has_after, give(64, 1, 0, (vol + 1, 0), edge_sem.at[3])),
    )
    for wanted, copy in edges:
        pl.when(wanted)(copy.start)

    def send(step, carry):
        for target in (lax.rem(me - step + members, members), lax.rem(me + 1 + step, members)):
            partial = (has_before & (target == 0)) | (has_after & (target == members - 1))

            @pl.when(jnp.logical_not(partial) & (target != me))
            def _():
                give(target, 3, 0, (vol, target), send_sem).start()

        return carry

    lax.fori_loop(0, 8, send, 0, unroll=4)

    def keep(start, count, slot):
        pltpu.make_async_copy(
            tiles.at[pl.ds(start, count)], got_ref.at[me, pl.ds(slot, count)], recv_sem.at[me]
        ).start()

    keep_first, keep_last = has_before & at_first, has_after & at_last
    pl.when(keep_first)(lambda: keep(1, 2, 1))
    pl.when(keep_last)(lambda: keep(63, 2, 0))
    pl.when(jnp.logical_not(keep_first | keep_last))(lambda: keep(me, 3, 0))

    for each in loads:
        each.wait()
    edge = jnp.where(
        (vol == 0) & at_first, 1, jnp.where((vol == vols - 1) & at_last, 2, 0)
    )
    lay_weights(edge, fetched[:8], fetched[8:], laid)
    lax.fori_loop(8, 16, send, 0, unroll=4)

    def arrive(turn):
        if isinstance(turn, int) and 16 + 4 * turn < HALF:
            lax.fori_loop(16 + 4 * turn, 16 + 4 * (turn + 1), send, 0, unroll=4)
        for half in range(2):
            step = 2 * turn + half
            for z in (lax.rem(me + step, members), lax.rem(me - 1 - step + 2 * members, members)):
                pltpu.make_async_copy(got_ref.at[z], got_ref.at[z], recv_sem.at[z]).wait()

    def leave(slot):
        pltpu.make_async_copy(out_ref.at[slot], out_hbm.at[slot], out_sem).start()

    convolve_slices(me, arrive, leave, got_ref, laid, held, out_ref)

    for wanted, copy in edges:
        pl.when(wanted)(copy.wait_send)
    partials = jnp.where(edges[0][0], 1, 0) + jnp.where(edges[2][0], 1, 0)
    for count in range(3):
        @pl.when(partials == count)
        def _():
            rest = got_ref.at[pl.ds(0, 63 - count)]
            pltpu.make_async_copy(rest, rest, send_sem).wait()
    pltpu.make_async_copy(out_ref, out_hbm, out_sem).wait()


def encode(volume, *raw):
    fetched = (*raw, *tables())
    return pl.pallas_call(
        encoder_kernel,
        out_shape=jax.ShapeDtypeStruct((DEPTH, 48, 128), BF16),
        in_specs=[pl.BlockSpec(memory_space=pltpu.HBM)] * 19,
        out_specs=pl.BlockSpec(memory_space=pltpu.HBM),
        scratch_shapes=[
            pltpu.VMEM(volume.shape, BF16),
            *[pltpu.VMEM(value.shape, value.dtype) for value in fetched],
            pltpu.VMEM((256, 80), BF16),
            pltpu.VMEM((192, 512), BF16),
            pltpu.VMEM((96, 192), BF16),
            pltpu.VMEM((96, 128), F32),
            pltpu.VMEM((144, 304), BF16),
            pltpu.VMEM((4, 512, 256), BF16),
            pltpu.VMEM((4, 192, 256), BF16),
            pltpu.VMEM((4, 304, 256), BF16),
            pltpu.VMEM((66, 8, 128), BF16),
            pltpu.VMEM((DEPTH, 3, 8, 128), BF16),
            pltpu.VMEM((DEPTH, 48, 128), BF16),
            pltpu.SemaphoreType.DMA((19,)),
            pltpu.SemaphoreType.DMA((4,)),
            pltpu.SemaphoreType.DMA,
            pltpu.SemaphoreType.DMA,
            pltpu.SemaphoreType.DMA((DEPTH,)),
        ],
        compiler_params=pltpu.CompilerParams(
            collective_id=0, has_side_effects=True, vmem_limit_bytes=56 * 1024 * 1024
        ),
        name="encode",
    )(volume, *fetched)


CHUNKS = 4


def hand_kernel(source, target, held, in_sem, out_sem):
    rows = DEPTH // CHUNKS
    parts = [pl.ds(at * rows, rows) for at in range(CHUNKS)]
    into = [
        pltpu.make_async_copy(source.at[part], held.at[part], in_sem.at[at])
        for at, part in enumerate(parts)
    ]
    out = [
        pltpu.make_async_copy(held.at[part], target.at[part], out_sem.at[at])
        for at, part in enumerate(parts)
    ]
    for copy in into:
        copy.start()
    for first, second in zip(into, out):
        first.wait()
        second.start()
    for copy in out:
        copy.wait()


def hand(done):
    return pl.pallas_call(
        hand_kernel,
        out_shape=jax.ShapeDtypeStruct(done.shape, BF16),
        in_specs=[pl.BlockSpec(memory_space=pltpu.HBM)],
        out_specs=pl.BlockSpec(memory_space=pltpu.HBM),
        scratch_shapes=[
            pltpu.VMEM(done.shape, BF16),
            pltpu.SemaphoreType.DMA((CHUNKS,)),
            pltpu.SemaphoreType.DMA((CHUNKS,)),
        ],
        compiler_params=pltpu.CompilerParams(vmem_limit_bytes=56 * 1024 * 1024),
        name="hand",
    )(done)


def shards(volume, w1, o1, w2, o2, w3, o3, w4, o4):
    done = encode(
        volume,
        w1,
        o1[None],
        w2,
        o2[None],
        w3.transpose(1, 0, 2),
        o3[None],
        w4.transpose(1, 2, 0),
        o4[None],
    )
    return hand(done).reshape(DEPTH, 24, 2, 128)


def solution(mesh):
    return jax.shard_map(
        shards,
        mesh=mesh,
        in_specs=(P("zs", "vol", None), P(), P(), P(), P(), P(), P(), P(), P()),
        out_specs=P(None, None, ("vol", "zs"), None),
        check_vma=False,
    )
```

```python
import functools

import jax
import jax.numpy as jnp
import numpy as np
from jax import lax
from jax.experimental import pallas as pl
from jax.experimental.pallas import tpu as pltpu
from jax.sharding import PartitionSpec as P

BF16 = jnp.bfloat16
F32 = jnp.float32
MESH = pl.DeviceIdType.MESH
DEPTH = 64
HALF = DEPTH // 2


def tables():
    place1 = np.zeros((3, 256, 12), np.float32)
    mask1 = np.zeros((256, 180), np.float32)
    pick1 = np.zeros((180, 9), np.float32)
    lay1 = np.zeros((180, 80), np.float32)
    source = ({0: (0, 1), 1: (1, 0), 2: (1, 1)}, {0: (1, 0), 1: (1, 1), 2: (2, 0)})
    for parity in range(2):
        for row in range(10):
            kind = parity * 10 + row
            for chan in range(12):
                at = parity * 128 + chan * 10 + row
                place1[0, at, chan] = 1
                place1[1, at, chan] = row >= 3
                place1[2, at, chan] = row < 7
                mask1[at, kind * 9 : kind * 9 + 9] = 1
            for along_x in range(3):
                for along_y in range(3):
                    tap = 3 * along_x + along_y
                    pick1[kind * 9 + tap, tap] = 1
                    shift, origin = source[parity][along_y]
                    fine = row + along_x
                    column = shift * 24 + (fine // 4) * 8 + origin * 4 + fine % 4
                    lay1[kind * 9 + tap, column] = 1
    place2 = np.zeros((96, 12), np.float32)
    lay2 = np.zeros((9, 12, 1024), np.float32)
    block = ({0: 0, 1: 1, 2: 2}, {0: 1, 1: 2, 2: 3})
    for chan in range(12):
        place2[chan * 8 : chan * 8 + 8, chan] = 1
        for along_x in range(3):
            for along_y in range(3):
                for parity in range(2):
                    column = parity * 512 + block[parity][along_y] * 128 + chan * 10 + along_x
                    lay2[3 * along_x + along_y, chan, column] = 1
    place3 = np.zeros((3, 96, 24), np.float32)
    for chan in range(24):
        for row in range(4):
            place3[0, chan * 4 + row, chan] = 1
            place3[1, chan * 4 + row, chan] = row >= 1
            place3[2, chan * 4 + row, chan] = row < 3
    lay3 = np.zeros((12, 4, 256), np.float32)
    for a in range(2):
        for b in range(2):
            for chan in range(12):
                lay3[chan, 2 * a + b, b * 96 + chan * 8 + a] = 1
    place4 = np.zeros((48, 24), np.float32)
    lay4 = np.zeros((24, 27, 1152), np.float32)
    for chan in range(24):
        place4[chan * 2 : chan * 2 + 2, chan] = 1
        for along_z in range(3):
            for along_x in range(3):
                for along_y in range(3):
                    tap = 9 * along_z + 3 * along_x + along_y
                    lay4[chan, tap, along_z * 384 + along_y * 96 + chan * 4 + along_x] = 1
    made = (place1, mask1, pick1, lay1, place2, lay2, place3, lay3, place4, lay4)
    return [table.astype(jnp.bfloat16) for table in made]


def mul(a, b):
    return jnp.dot(a, b, preferred_element_type=F32)


def mul_t(a, b):
    return lax.dot_general(a, b, (((1,), (1,)), ((), ())), preferred_element_type=F32)


def column(place, offset):
    return jnp.sum(place.astype(F32) * offset, axis=1, keepdims=True)


def with_bias(weight, bias, start):
    high = bias.astype(BF16).astype(F32)
    middle = (bias - high).astype(BF16).astype(F32)
    low = bias - high - middle
    lane = lax.broadcasted_iota(jnp.int32, weight.shape, 1)
    for shift, part in enumerate((high, middle, low)):
        weight = jnp.where(lane == start + shift, part, weight)
    return weight.astype(BF16)


def lay_weights(edge, raw, consts, laid):
    w1_ref, o1_ref, w2_ref, o2_ref, w3_ref, o3_ref, w4_ref, o4_ref = raw
    place1, mask1, pick1, lay1, place2, lay2, place3, lay3, place4, lay4 = consts
    m1, m2, m3, b3, m4 = laid

    here1, here2, here3 = place1[edge], place2[...], place3[edge]
    taps1 = mul(pick1[...], w1_ref[...]).astype(BF16)
    taps2 = [mul_t(here2, w2_ref[tap]).astype(BF16) for tap in range(9)]
    taps3 = [mul_t(here3, w3_ref[chan]).astype(BF16) for chan in range(12)]
    wide4 = sum(mul(w4_ref[chan], lay4[chan]) for chan in range(24)).astype(BF16)

    chosen = mul_t(here1, taps1) * mask1[...].astype(F32)
    base2 = sum(mul(taps2[tap], lay2[tap]) for tap in range(9))
    base3 = sum(mul(taps3[chan], lay3[chan]) for chan in range(12))
    base4 = mul(place4[...], wide4)

    row = lax.broadcasted_iota(jnp.int32, (256, 1), 0) & 127
    bias1 = jnp.where(row >= 120, 1.0, column(here1, o1_ref[...]))
    m1[...] = with_bias(mul(chosen.astype(BF16), lay1[...]), bias1, 72)
    bias2 = column(here2, o2_ref[...])
    for parity in range(2):
        for block in range(4):
            start = parity * 512 + block * 128
            rows = [
                pltpu.roll(base2[8 * c : 8 * c + 8, start : start + 128], 0, 1, stride=1, stride_axis=0)
                for c in range(12)
            ]
            placed = jnp.concatenate(rows, axis=0)
            placed = with_bias(placed, bias2, 120) if block == 1 else placed.astype(BF16)
            m2[96 * parity : 96 * parity + 96, 128 * block : 128 * block + 128] = placed
    row = lax.broadcasted_iota(jnp.int32, base3.shape, 0) & 3
    placed = base3
    for r in range(1, 4):
        placed = jnp.where(row == r, pltpu.roll(base3, 2 * r, 1), placed)
    m3[...] = placed[:, :192].astype(BF16)
    row = lax.broadcasted_iota(jnp.int32, base4.shape, 0) & 1
    placed = jnp.where(row == 1, pltpu.roll(base4, 1, 1), base4)
    bias4 = column(place4[...], o4_ref[...])
    for dz in range(3):
        part = placed[:, 384 * dz : 384 * dz + 304]
        part = with_bias(part, bias4, 288) if dz == 1 else part.astype(BF16)
        m4[48 * dz : 48 * dz + 48] = part
    b3[...] = jnp.broadcast_to(column(here3, o3_ref[...]), (96, 128))


def from_left(value, lane):
    return jnp.where(lane == 0, jnp.zeros((), BF16), pltpu.roll(value, 1, 1))


def from_right(value, lane):
    return jnp.where(lane == 127, jnp.zeros((), BF16), pltpu.roll(value, 127, 1))


def both(function, value):
    lane = lax.broadcasted_iota(jnp.int32, (value.shape[0], 128), 1)
    return jnp.concatenate([function(value[:, :128], lane), function(value[:, 128:], lane)], axis=1)


def twice(bias):
    return jnp.concatenate([bias, bias], axis=1)


def relu(value):
    return jnp.maximum(value.astype(BF16), jnp.zeros((), BF16))


def swap(value):
    return jnp.concatenate([value[:, 128:], value[:, :128]], axis=1)


def place_first(x_ref, m1, first_ref, lows, spot):
    for half, (low, high) in enumerate(lows):
        field = jnp.concatenate(
            [x_ref[low].astype(F32).reshape(24, 128), x_ref[high].astype(F32).reshape(24, 128)], axis=1
        )
        lane = lax.broadcasted_iota(jnp.int32, field.shape, 1) & 127
        before = jnp.concatenate(
            [pltpu.roll(field[:, :128], 1, 1), pltpu.roll(field[:, 128:], 1, 1)], axis=1
        )
        after = jnp.concatenate(
            [pltpu.roll(field[:, :128], 127, 1), pltpu.roll(field[:, 128:], 127, 1)], axis=1
        )
        before = jnp.where(lane == 0, 0.0, before)
        after = jnp.where(lane == 127, 0.0, after)
        stacked = jnp.concatenate([before, field, after, jnp.ones((8, 256), F32)], axis=0)
        first = relu(mul(m1[...], stacked.astype(BF16)))
        even, odd = first[:128], first[128:]
        first_ref[spot + half, :128] = both(from_left, odd)
        first_ref[spot + half, 128:256] = even
        first_ref[spot + half, 256:384] = odd
        first_ref[spot + half, 384:] = both(from_right, even)


def place_second(first_ref, m2, second_ref, spot):
    for at in (spot, spot + 1):
        second_ref[at] = relu(mul(m2[...], first_ref[at]))


def place_coarse(second_ref, m3, b3, coarse_ref, spot):
    for at in (spot, spot + 1):
        coarse = relu(mul(m3[...], second_ref[at]) + twice(b3[...]))
        coarse_ref[at, :96] = both(from_left, coarse)
        coarse_ref[at, 96:192] = coarse
        coarse_ref[at, 192:288] = both(from_right, coarse)


def convolve_slices(me, arrive, leave, x_ref, laid, held, out_ref):
    m1, m2, m3, b3, m4 = laid
    first_ref, second_ref, coarse_ref = held
    coarse_ref[:, 288:] = jnp.ones((4, 16, 256), BF16)
    groups = HALF // 2

    def up(step):
        return lax.rem(me + step, DEPTH)

    def down(step):
        return lax.rem(me - 1 - step + 2 * DEPTH, DEPTH)

    def stage1(turn, odd):
        pairs = [(up(2 * turn + half), down(2 * turn + half)) for half in range(2)]
        place_first(x_ref, m1, first_ref, pairs, 2 * odd)

    def stage2(odd):
        place_second(first_ref, m2, second_ref, 2 * odd)

    def stage3(odd):
        place_coarse(second_ref, m3, b3, coarse_ref, 2 * odd)

    def joined(step, part):
        low = jnp.where(up(step) == 0, 0.0, part[:, :128])
        return jnp.concatenate([low, jnp.where(down(step) == DEPTH - 1, 0.0, part[:, 128:])], axis=1)

    def emit(step, total):
        done = relu(total)
        out_ref[up(step)] = done[:, :128]
        out_ref[down(step)] = done[:, 128:]
        leave(up(step))
        leave(down(step))

    def stage4(group, odd, carry):
        for half in range(2):
            step = 2 * group + half
            deep = mul(m4[...], coarse_ref[2 * odd + half])
            here = deep[48:96]
            back = jnp.concatenate([deep[96:, :128], deep[:48, 128:]], axis=1)
            forth = jnp.concatenate([deep[:48, :128], deep[96:, 128:]], axis=1)
            if carry is None:
                carry = here + jnp.where(me == 0, 0.0, swap(back)), forth
            else:
                closing, opening = carry
                emit(step - 1, closing + joined(step, back))
                carry = here + joined(step, opening), forth
        return carry

    arrive(0)
    stage1(0, 0)
    arrive(1)
    stage2(0)
    stage1(1, 1)
    arrive(2)
    stage3(0)
    stage2(1)
    stage1(2, 0)
    arrive(3)
    carry = stage4(0, 0, None)
    stage3(1)
    stage2(0)
    stage1(3, 1)

    def step(turn, carry):
        for more in range(2):
            arrive(4 + 2 * turn + more)
        for more in range(2):
            stage1(4 + 2 * turn + more, more)
            stage2(1 - more)
            stage3(more)
            carry = stage4(1 + 2 * turn + more, 1 - more, carry)
        return carry

    carry = lax.fori_loop(0, (groups - 6) // 2, step, carry)
    arrive(groups - 2)
    carry = stage4(groups - 5, 1, carry)
    stage3(0)
    stage2(1)
    stage1(groups - 2, 0)
    arrive(groups - 1)
    stage1(groups - 1, 1)
    carry = stage4(groups - 4, 0, carry)
    stage2(0)
    stage3(1)
    stage2(1)
    stage3(0)
    carry = stage4(groups - 3, 1, carry)
    stage3(1)
    carry = stage4(groups - 2, 0, carry)
    closing, opening = stage4(groups - 1, 1, carry)
    emit(HALF - 1, closing + jnp.where(me == HALF, 0.0, swap(opening)))


def encoder_kernel(*refs):
    volume_hbm, fetched_hbm, out_hbm = refs[0], refs[1:19], refs[19]
    volume_ref, fetched = refs[20], refs[21:39]
    laid, held = refs[39:44], refs[44:47]
    tiles, got_ref, out_ref = refs[47:50]
    fetch_sem, edge_sem, send_sem, out_sem, recv_sem = refs[50:]
    vol, me = lax.axis_index("vol"), lax.axis_index("zs")
    vols, members = lax.axis_size("vol"), lax.axis_size("zs")
    has_before, has_after = vol > 0, vol < vols - 1
    at_first, at_last = me == 0, me == members - 1

    load = pltpu.make_async_copy(volume_hbm, volume_ref, fetch_sem.at[18])
    load.start()
    loads = [
        pltpu.make_async_copy(source, target, fetch_sem.at[at])
        for at, (source, target) in enumerate(zip(fetched_hbm, fetched))
    ]
    barrier = pltpu.get_barrier_semaphore()

    def signal(vol_index, member):
        pl.semaphore_signal(barrier, inc=1, device_id=(vol_index, member), device_id_type=MESH)

    def greet(member, carry):
        pl.when(member != me)(lambda: signal(vol, member))
        return carry

    def greet_before(member, carry):
        signal(vol - 1, member)
        return carry

    def greet_after(member, carry):
        signal(vol + 1, member)
        return carry

    lax.fori_loop(0, members, greet, 0, unroll=8)

    @pl.when(has_before & at_first)
    def _():
        lax.fori_loop(0, members, greet_before, 0, unroll=8)

    @pl.when(has_after & at_last)
    def _():
        lax.fori_loop(0, members, greet_after, 0, unroll=8)

    for each in loads:
        each.start()
    load.wait()

    line = lax.broadcasted_iota(jnp.int32, (256, 256), 0)
    lane = lax.broadcasted_iota(jnp.int32, (256, 256), 1)
    parted = (line == jnp.where(lane < 128, 2 * lane, 2 * lane - 255)).astype(F32).astype(BF16)
    split = mul(volume_ref[0], parted)
    even = split[:, :128].reshape(32, 8, 128)
    odd = split[:, 128:].reshape(32, 8, 128)
    row = lax.broadcasted_iota(jnp.int32, (32, 8, 128), 1)
    upper = jnp.where(row < 4, even, pltpu.roll(odd, 4, 1))
    lower = jnp.where(row < 4, pltpu.roll(even, 4, 1), odd)
    tiles[1:65] = jnp.stack([upper, lower], axis=1).reshape(64, 8, 128).astype(BF16)

    tiles[0] = jnp.zeros((8, 128), BF16)
    tiles[65] = jnp.zeros((8, 128), BF16)

    pl.semaphore_wait(
        barrier, members - 1 + jnp.where(has_before, 1, 0) + jnp.where(has_after, 1, 0)
    )

    def give(start, count, slot, to, sem):
        return pltpu.make_async_remote_copy(
            src_ref=tiles.at[pl.ds(start, count)],
            dst_ref=got_ref.at[me, pl.ds(slot, count)],
            send_sem=sem,
            recv_sem=recv_sem.at[me],
            device_id=to,
            device_id_type=MESH,
        )

    edges = (
        (has_before & jnp.logical_not(at_first), give(1, 2, 1, (vol, 0), edge_sem.at[0])),
        (has_before, give(1, 1, 2, (vol - 1, members - 1), edge_sem.at[1])),
        (has_after & jnp.logical_not(at_last), give(63, 2, 0, (vol, members - 1), edge_sem.at[2])),
        (has_after, give(64, 1, 0, (vol + 1, 0), edge_sem.at[3])),
    )
    for wanted, copy in edges:
        pl.when(wanted)(copy.start)

    def send(step, carry):
        for target in (lax.rem(me - step + members, members), lax.rem(me + 1 + step, members)):
            partial = (has_before & (target == 0)) | (has_after & (target == members - 1))

            @pl.when(jnp.logical_not(partial) & (target != me))
            def _():
                give(target, 3, 0, (vol, target), send_sem).start()

        return carry

    lax.fori_loop(0, 8, send, 0, unroll=4)

    def keep(start, count, slot):
        pltpu.make_async_copy(
            tiles.at[pl.ds(start, count)], got_ref.at[me, pl.ds(slot, count)], recv_sem.at[me]
        ).start()

    keep_first, keep_last = has_before & at_first, has_after & at_last
    pl.when(keep_first)(lambda: keep(1, 2, 1))
    pl.when(keep_last)(lambda: keep(63, 2, 0))
    pl.when(jnp.logical_not(keep_first | keep_last))(lambda: keep(me, 3, 0))

    for each in loads:
        each.wait()
    edge = jnp.where(
        (vol == 0) & at_first, 1, jnp.where((vol == vols - 1) & at_last, 2, 0)
    )
    lay_weights(edge, fetched[:8], fetched[8:], laid)
    lax.fori_loop(8, 16, send, 0, unroll=4)

    def arrive(turn):
        if isinstance(turn, int) and 16 + 4 * turn < HALF:
            lax.fori_loop(16 + 4 * turn, 16 + 4 * (turn + 1), send, 0, unroll=4)
        for half in range(2):
            step = 2 * turn + half
            for z in (lax.rem(me + step, members), lax.rem(me - 1 - step + 2 * members, members)):
                pltpu.make_async_copy(got_ref.at[z], got_ref.at[z], recv_sem.at[z]).wait()

    def leave(slot):
        pltpu.make_async_copy(out_ref.at[slot], out_hbm.at[slot], out_sem).start()

    convolve_slices(me, arrive, leave, got_ref, laid, held, out_ref)

    for wanted, copy in edges:
        pl.when(wanted)(copy.wait_send)
    partials = jnp.where(edges[0][0], 1, 0) + jnp.where(edges[2][0], 1, 0)
    for count in range(3):
        @pl.when(partials == count)
        def _():
            rest = got_ref.at[pl.ds(0, 63 - count)]
            pltpu.make_async_copy(rest, rest, send_sem).wait()
    pltpu.make_async_copy(out_ref, out_hbm, out_sem).wait()


def encode(volume, *raw):
    fetched = (*raw, *tables())
    return pl.pallas_call(
        encoder_kernel,
        out_shape=jax.ShapeDtypeStruct((DEPTH, 48, 128), BF16),
        in_specs=[pl.BlockSpec(memory_space=pltpu.HBM)] * 19,
        out_specs=pl.BlockSpec(memory_space=pltpu.HBM),
        scratch_shapes=[
            pltpu.VMEM(volume.shape, BF16),
            *[pltpu.VMEM(value.shape, value.dtype) for value in fetched],
            pltpu.VMEM((256, 80), BF16),
            pltpu.VMEM((192, 512), BF16),
            pltpu.VMEM((96, 192), BF16),
            pltpu.VMEM((96, 128), F32),
            pltpu.VMEM((144, 304), BF16),
            pltpu.VMEM((4, 512, 256), BF16),
            pltpu.VMEM((4, 192, 256), BF16),
            pltpu.VMEM((4, 304, 256), BF16),
            pltpu.VMEM((66, 8, 128), BF16),
            pltpu.VMEM((DEPTH, 3, 8, 128), BF16),
            pltpu.VMEM((DEPTH, 48, 128), BF16),
            pltpu.SemaphoreType.DMA((19,)),
            pltpu.SemaphoreType.DMA((4,)),
            pltpu.SemaphoreType.DMA,
            pltpu.SemaphoreType.DMA,
            pltpu.SemaphoreType.DMA((DEPTH,)),
        ],
        compiler_params=pltpu.CompilerParams(
            collective_id=0, has_side_effects=True, vmem_limit_bytes=56 * 1024 * 1024
        ),
        name="encode",
    )(volume, *fetched)


CHUNKS = 4


def hand_kernel(source, target, held, in_sem, out_sem):
    rows = DEPTH // CHUNKS
    parts = [pl.ds(at * rows, rows) for at in range(CHUNKS)]
    into = [
        pltpu.make_async_copy(source.at[part], held.at[part], in_sem.at[at])
        for at, part in enumerate(parts)
    ]
    out = [
        pltpu.make_async_copy(held.at[part], target.at[part], out_sem.at[at])
        for at, part in enumerate(parts)
    ]
    for copy in into:
        copy.start()
    for first, second in zip(into, out):
        first.wait()
        second.start()
    for copy in out:
        copy.wait()


def hand(done):
    return pl.pallas_call(
        hand_kernel,
        out_shape=jax.ShapeDtypeStruct(done.shape, BF16),
        in_specs=[pl.BlockSpec(memory_space=pltpu.HBM)],
        out_specs=pl.BlockSpec(memory_space=pltpu.HBM),
        scratch_shapes=[
            pltpu.VMEM(done.shape, BF16),
            pltpu.SemaphoreType.DMA((CHUNKS,)),
            pltpu.SemaphoreType.DMA((CHUNKS,)),
        ],
        compiler_params=pltpu.CompilerParams(vmem_limit_bytes=56 * 1024 * 1024),
        name="hand",
    )(done)


def shards(volume, w1, o1, w2, o2, w3, o3, w4, o4):
    done = encode(
        volume,
        w1,
        o1[None],
        w2,
        o2[None],
        w3.transpose(1, 0, 2),
        o3[None],
        w4.transpose(1, 2, 0),
        o4[None],
    )
    return hand(done).reshape(DEPTH, 24, 2, 128)


def solution(mesh):
    return jax.shard_map(
        shards,
        mesh=mesh,
        in_specs=(P("zs", "vol", None), P(), P(), P(), P(), P(), P(), P(), P()),
        out_specs=P(None, None, ("vol", "zs"), None),
        check_vma=False,
    )
```
